512 devices in a mesh: section: 32 (over y, z_hi), tp: 16 (over z_lo, x, core).
Axes of the slice: x: 4, y: 8, z: 8 (z_hi: 4, z_lo: 2; z = z_hi * 2 + z_lo), core: 2. Of those that a mesh axis runs over, the one named last changes fastest.
Arguments:
- carried_acts: bfloat16 [32, 2, 32, 4096], P('section', None, 'tp'), may hold values from -6 to 6
- fresh_acts: bfloat16 [2, 1, 32, 4096], P(None, None, 'tp'), may hold values from -6 to 6
- stashed_acts: bfloat16 [32, 2, 2, 32, 4096], P('section', None, None, 'tp'), may hold values from -6 to 6
- carried_grads: bfloat16 [32, 2, 32, 4096], P('section', None, 'tp'), may hold values from -6 to 6
- fresh_grads: bfloat16 [2, 1, 32, 4096], P(None, None, 'tp'), may hold values from -6 to 6
- norm_gain: bfloat16 [32, 2048], P('section'), may hold values from 0.59765625 to 1.3984375
- query_weight: bfloat16 [32, 2048, 4096], P('section', None, 'tp'), may hold values from -0.09375 to 0.09375
- keyval_weight: bfloat16 [32, 2048, 1024], P('section', None, 'tp'), may hold values from -0.09375 to 0.09375
- output_weight: bfloat16 [32, 4096, 2048], P('section', 'tp'), may hold values from -0.09375 to 0.09375
Outputs:
- layer_outputs: bfloat16 [32, 2, 2, 32, 4096], P('section', None, None, 'tp')
- input_grads: bfloat16 [32, 2, 2, 32, 4096], P('section', None, None, 'tp')
- grad_query: bfloat16 [32, 2048, 4096], P('section', None, 'tp')
- grad_keyval: bfloat16 [32, 2048, 1024], P('section', None, 'tp')
- grad_output: bfloat16 [32, 2048, 4096], P('section', None, 'tp')
- grad_gain: bfloat16 [32, 2048], P('section')
The draws below stay inside these ranges and needn't reach their ends.
All inputs are finite; a program needn't handle non-finite values.
Results may differ from the reference program's by a relative error of at most 0.035.
Values may be sent and summed in bfloat16 or wider, within the bound.
No kernel may reach another device: no remote copies, remote signals or barrier semaphores. Data moves between devices by JAX's collectives and lax.ppermute only.
A program may use at most 64 MiB of HBM per device.

```python
import math
import jax
import jax.numpy as jnp
from jax import lax

D = 4096
HD = 128
KVH = 4
TOK = 32
TICKS = 2
HEADS = 32
N_SECTION = 32
N_TP = 16


def block_levels(key, extent, shards, smallest, top_value):
    def one(dim, blocks):
        draws = jax.random.uniform(jax.random.fold_in(jax.random.fold_in(key, 6), dim), (blocks,), jnp.float32, smallest / len(shards), top_value / len(shards))
        return jnp.repeat(jnp.exp(draws), extent[dim] // blocks).reshape((-1,) + (1,) * (len(extent) - dim - 1))

    level = one(*shards[0])
    for cut in shards[1:]:
        level = level * one(*cut)
    return level


def noise(key, shape, deviation, reach, split=(), dtype=jnp.bfloat16):
    level = block_levels(key, shape, split, -0.22, 0.18) if split else 1.0
    values = jax.random.normal(key, shape, jnp.float32) * deviation * level
    return jnp.minimum(jnp.maximum(values, -reach), reach).astype(dtype)


def setup_inputs(seed: int = 0) -> dict:
    splits = jax.random.split(jax.random.key(seed), 10)
    carried_acts = noise(splits[0], (N_SECTION, 2, TOK, D), 1.0, 6.0, ((0, 32), (2, 16)))
    fresh_acts = noise(splits[1], (2, TICKS - 1, TOK, D), 1.0, 6.0, ((2, 16),))
    stashed_acts = noise(splits[2], (N_SECTION, 2, TICKS, TOK, D), 1.0, 6.0, ((0, 32), (3, 16)))
    carried_grads = noise(splits[3], (N_SECTION, 2, TOK, D), 1.0, 6.0, ((0, 32), (2, 16)))
    fresh_grads = noise(splits[4], (2, TICKS - 1, TOK, D), 1.0, 6.0, ((2, 16),))
    norm_gain = jnp.clip(1.0 + 0.08 * jax.random.normal(splits[5], (N_SECTION, D // 2), jnp.float32), 0.59765625, 1.3984375).astype(jnp.bfloat16)
    query_weight = noise(splits[6], (N_SECTION, D // 2, HEADS * HD), D ** -0.5, 0.09375, ((0, 32), (2, 16)))
    keyval_weight = noise(splits[7], (N_SECTION, D // 2, 2 * KVH * HD), D ** -0.5, 0.09375, ((0, 32), (2, 16)))
    output_weight = noise(splits[8], (N_SECTION, HEADS * HD, D // 2), (HEADS * HD) ** -0.5, 0.09375, ((0, 32), (1, 16)))
    return {"carried_acts": carried_acts, "fresh_acts": fresh_acts, "stashed_acts": stashed_acts, "carried_grads": carried_grads, "fresh_grads": fresh_grads, "norm_gain": norm_gain, "query_weight": query_weight, "keyval_weight": keyval_weight, "output_weight": output_weight}


EPSILON = 1e-05

def normalize(value_rows, gain):
    widened = value_rows.astype(jnp.float32)
    inverse = lax.rsqrt(lax.optimization_barrier(jnp.mean(widened * widened, axis=-1, keepdims=True)) + EPSILON)
    unit = widened * inverse
    return (unit, inverse, (unit * gain.astype(jnp.float32)).astype(jnp.bfloat16))

def project(left, right):
    return jnp.einsum('dtk,kc->dtc', left.astype(jnp.float32), right.astype(jnp.float32)).astype(jnp.bfloat16)

def softmax_rows(queries, keys):
    tokens = queries.shape[1]
    causal = jnp.arange(tokens)[:, None] >= jnp.arange(tokens)[None, :]
    scores = jnp.einsum('dthe,dshe->dhts', queries, keys, precision=lax.Precision.HIGHEST) / math.sqrt(queries.shape[-1])
    scores = jnp.where(causal, scores, -jnp.inf)
    weights = jnp.exp(scores - lax.optimization_barrier(jnp.max(scores, axis=-1, keepdims=True)))
    return weights / lax.optimization_barrier(jnp.sum(weights, axis=-1, keepdims=True))

def split_heads(packed):
    tokens = packed.shape[1]
    keys = packed[..., :KVH * HD].reshape(2, tokens, KVH, HD).astype(jnp.float32)
    value_rows = packed[..., KVH * HD:].reshape(2, tokens, KVH, HD).astype(jnp.float32)
    return (keys, value_rows)

def attention_out(queries, keys, value_rows, groups):
    attention_probabilities = softmax_rows(queries, jnp.repeat(keys, groups, axis=2)).astype(jnp.bfloat16)
    mixed = jnp.einsum('dhts,dshe->dthe', attention_probabilities.astype(jnp.float32), jnp.repeat(value_rows, groups, axis=2), precision=lax.Precision.HIGHEST)
    return mixed.astype(jnp.bfloat16).reshape(2, queries.shape[1], -1)

def attention_exact(queries, keys, value_rows, groups):
    attention_probabilities = softmax_rows(queries, jnp.repeat(keys, groups, axis=2))
    return jnp.einsum('dhts,dshe->dthe', attention_probabilities, jnp.repeat(value_rows, groups, axis=2), precision=lax.Precision.HIGHEST)

def shard_sum(terms):
    total = None
    for left, right in terms:
        tokens = left.shape[1]
        piece = jnp.einsum('dtjc,jck->jdtk', left.reshape(2, tokens, N_TP, -1).astype(jnp.float32), right.reshape(N_TP, -1, right.shape[-1]).astype(jnp.float32))
        total = piece if total is None else total + piece
    rounded = lax.optimization_barrier(total.astype(jnp.bfloat16))
    return lax.optimization_barrier(jnp.sum(rounded.astype(jnp.float32), axis=0))

def attention_inputs(current, gain, query_mat, keyval_mat):
    unit, inverse, normed = normalize(current, gain)
    tokens = current.shape[1]
    heads = query_mat.shape[1] // HD
    queries = project(normed, query_mat).reshape(2, tokens, heads, HD).astype(jnp.float32)
    keys, value_rows = split_heads(project(normed, keyval_mat))
    return (unit, inverse, normed, queries, keys, value_rows, heads // KVH)

def layer_forward(current, gain, query_mat, keyval_mat, output_mat):
    unit, inverse, normed, queries, keys, value_rows, groups = attention_inputs(current, gain, query_mat, keyval_mat)
    mixed = attention_out(queries, keys, value_rows, groups)
    total = shard_sum(((mixed, output_mat),))
    return (current.astype(jnp.float32) + total).astype(jnp.bfloat16)

def layer_backward(current, upstream, gain, query_mat, keyval_mat, output_mat):
    unit, inverse, normed, queries, keys, value_rows, groups = attention_inputs(current, gain, query_mat, keyval_mat)
    tokens = current.shape[1]
    mixed = attention_out(queries, keys, value_rows, groups)
    back_mixed = project(upstream, output_mat.T)

    def exact(query_part, key_part, value_part):
        return attention_exact(query_part, key_part, value_part, groups)
    unused, pullback = jax.vjp(exact, queries, keys, value_rows)
    grad_heads, key_gradients, grad_values = pullback(back_mixed.reshape(queries.shape).astype(jnp.float32))
    query_back = grad_heads.reshape(2, tokens, -1).astype(jnp.bfloat16)
    keyval_back = jnp.concatenate([key_gradients.reshape(2, tokens, -1), grad_values.reshape(2, tokens, -1)], axis=-1).astype(jnp.bfloat16)
    grad_query = jnp.einsum('dtk,dtc->kc', normed.astype(jnp.float32), query_back.astype(jnp.float32))
    grad_keyval = jnp.einsum('dtk,dtc->kc', normed.astype(jnp.float32), keyval_back.astype(jnp.float32))
    grad_output = jnp.einsum('dtk,dtc->kc', upstream.astype(jnp.float32), mixed.astype(jnp.float32))
    back_normed = shard_sum(((query_back, query_mat.T), (keyval_back, keyval_mat.T)))
    scaled = back_normed * gain.astype(jnp.float32)
    grad_gain = lax.optimization_barrier(jnp.sum(back_normed * unit, axis=(0, 1)))
    back_input = upstream.astype(jnp.float32) + inverse * (scaled - unit * lax.optimization_barrier(jnp.mean(scaled * unit, axis=-1, keepdims=True)))
    return (back_input.astype(jnp.bfloat16), grad_query, grad_keyval, grad_output, grad_gain)

def to_half(value_rows):
    return value_rows.astype(jnp.bfloat16)

def pair_sum(partial_grad):
    return (partial_grad.astype(jnp.float32) + partial_grad[::-1].astype(jnp.float32)).astype(jnp.bfloat16)

def whole_layer(halves, axis):
    lower = halves[:N_SECTION // 2]
    upper = halves[N_SECTION // 2:][::-1]
    joined = jnp.concatenate([lower, upper], axis=axis)
    return jnp.concatenate([joined, joined[::-1]], axis=0)

def kept_half(summed, axis):
    half = summed.shape[axis] // 2
    lower = lax.slice_in_dim(summed[:N_SECTION // 2], 0, half, axis=axis)
    upper = lax.slice_in_dim(summed[N_SECTION // 2:], half, 2 * half, axis=axis)
    return jnp.concatenate([lower, upper], axis=0)

def reference(carried_acts, fresh_acts, stashed_acts, carried_grads, fresh_grads, norm_gain, query_weight, keyval_weight, output_weight):
    ticks = stashed_acts.shape[2]
    layers = (whole_layer(norm_gain, 1), whole_layer(query_weight, 1), whole_layer(keyval_weight, 1), whole_layer(output_weight, 2))

    def forward_section(operands):
        return layer_forward(*operands)
    outputs = []
    current = carried_acts
    for tick_index in range(ticks):
        produced = lax.map(forward_section, (current,) + layers)
        outputs.append(produced)
        if tick_index + 1 < ticks:
            down = jnp.concatenate([fresh_acts[0, tick_index][None], produced[:-1, 0]], axis=0)
            upward = jnp.concatenate([produced[1:, 1], fresh_acts[1, tick_index][None]], axis=0)
            current = jnp.stack([down, upward], axis=1)

    def back_section(operands):
        return layer_backward(*operands)[0]
    cotangents = [carried_grads]
    current = carried_grads
    for tick_index in range(ticks - 1):
        backs = lax.map(back_section, (stashed_acts[:, :, tick_index], current) + layers)
        down = jnp.concatenate([backs[1:, 0], fresh_grads[0, tick_index][None]], axis=0)
        upward = jnp.concatenate([fresh_grads[1, tick_index][None], backs[:-1, 1]], axis=0)
        current = jnp.stack([down, upward], axis=1)
        cotangents.append(current)
    all_cotangents = jnp.stack(cotangents, axis=2)

    def section_sum_values(operands):
        held, upstream, gain, query_mat, keyval_mat, output_mat = operands
        backs = []
        totals = None
        for tick_index in range(ticks):
            result = layer_backward(held[:, tick_index], upstream[:, tick_index], gain, query_mat, keyval_mat, output_mat)
            backs.append(result[0])
            totals = result[1:] if totals is None else jax.tree.map(jnp.add, totals, result[1:])
        return (jnp.stack(backs, axis=1), jax.tree.map(to_half, totals))
    input_grads, partials = lax.map(section_sum_values, (stashed_acts, all_cotangents) + layers)
    summed = tuple((kept_half(pair_sum(partial_grad), 1) for partial_grad in partials))
    return (jnp.stack(outputs, axis=2), input_grads, summed[0], summed[1], summed[2], summed[3])
```

```python
import math

import jax
import jax.numpy as jnp
from jax import lax
from jax.sharding import PartitionSpec as P

HD = 128
KVH = 4
EPSILON = 1e-05
BF = jnp.bfloat16
F32 = jnp.float32


def mm(left, right, dims=((1,), (0,))):
    return lax.dot_general(left, right, (dims, ((), ())), preferred_element_type=F32)


def mm_t(left, right):
    return mm(left, right, ((1,), (1,)))


def t_mm(left, right):
    return mm(left, right, ((0,), (0,)))


def split_f32(values):
    high = values.astype(BF)
    return high, (values - high.astype(F32)).astype(BF)


def pair_mask(tokens):
    def parts(axis):
        i = lax.broadcasted_iota(jnp.int32, (tokens, tokens), axis)
        return (i // 2) % 4, (i // 8) * 2 + i % 2

    (query_group, query_time), (key_group, key_time) = parts(0), parts(1)
    return (query_group == key_group) & (key_time <= query_time)


def stack_heads(columns):
    return jnp.concatenate([columns[:, i : i + HD] for i in range(0, columns.shape[1], HD)], axis=0)


def unstack_heads(rows, tokens):
    return jnp.concatenate(
        [rows[i : i + tokens] for i in range(0, rows.shape[0], tokens)], axis=1
    )


def attention(queries, keyvals, mask):
    tokens = queries.shape[0]
    stacked, keys, values = stack_heads(queries), keyvals[:, :HD], keyvals[:, HD:]
    scores = mm_t(stacked, keys) / math.sqrt(HD)
    scores = jnp.where(jnp.concatenate([mask] * (queries.shape[1] // HD), 0), scores, -jnp.inf)
    weights = jnp.exp(scores - jnp.max(scores, axis=-1, keepdims=True))
    probs = weights / jnp.sum(weights, axis=-1, keepdims=True)
    mixed = mm(probs.astype(BF), values).astype(BF)
    return probs, unstack_heads(mixed, tokens)


def attention_back(queries, keyvals, probs, back_mixed):
    tokens = queries.shape[0]
    stacked, keys, values = stack_heads(queries), keyvals[:, :HD], keyvals[:, HD:]
    back = stack_heads(back_mixed)
    back_probs = mm_t(back, values)
    inner = jnp.sum(probs * back_probs, axis=-1, keepdims=True)
    back_scores = (probs * (back_probs - inner) / math.sqrt(HD)).astype(BF)
    query_back = unstack_heads(mm(back_scores, keys).astype(BF), tokens)
    key_back = t_mm(back_scores, stacked).astype(BF)
    value_back = t_mm(probs.astype(BF), back).astype(BF)
    return query_back, jnp.concatenate([key_back, value_back], axis=1)


def on_device(
    carried_acts,
    fresh_acts,
    stashed_acts,
    carried_grads,
    fresh_grads,
    norm_gain,
    query_weight,
    keyval_weight,
    output_weight,
):
    sections = lax.axis_size("section")
    shards = lax.axis_size("tp")
    section = lax.axis_index("section")
    me = lax.axis_index("tp")
    lower = section < sections // 2
    ticks = stashed_acts.shape[2]
    width = carried_acts.shape[3]
    half = width // 2
    row_count = carried_acts.shape[2]
    rows = 4 * row_count
    tokens = rows * shards
    gain = norm_gain[0].astype(F32)
    query_mat, output_mat = query_weight[0], output_weight[0]
    mirror = [(i, sections - 1 - i) for i in range(sections)]
    kv_group = shards // KVH

    def halves(whole):
        first, second = whole[..., :half], whole[..., half:]
        return jnp.where(lower, first, second), jnp.where(lower, second, first)

    kv_own = keyval_weight[0].T
    sources = [[2 * j, 2 * j + 1, shards // 2 + 2 * j, shards // 2 + 2 * j + 1] for j in range(KVH)]
    turned = [
        lax.ppermute(
            kv_own,
            "tp",
            [
                (sources[j][(i + k) % kv_group], kv_group * j + i)
                for j in range(KVH)
                for i in range(kv_group)
            ],
        )
        for k in range(kv_group)
    ]

    entering = jnp.stack(
        [carried_acts[0]] + [stashed_acts[0, :, k] for k in range(ticks)] + [carried_grads[0]]
    ).reshape(ticks + 2, 2 * row_count, width)
    own, other = halves(entering)
    arrived = lax.ppermute(other, "section", mirror)
    held = jnp.concatenate(
        [jnp.where(lower, own, arrived), jnp.where(lower, arrived, own)], axis=1
    )

    def gather(local):
        count = local.shape[0]
        spread = jnp.broadcast_to(local.reshape(1, count * rows, half), (shards, count * rows, half))
        full = lax.all_to_all(spread, "tp", split_axis=0, concat_axis=0, tiled=True)
        full = full.reshape(shards, count, rows, half)
        return [full[:, i].reshape(tokens, half) for i in range(count)]

    gathered = gather(held)
    acts, stash, cots = gathered[0], gathered[1 : 1 + ticks], gathered[1 + ticks]

    stacked_blocks = jnp.stack(turned)
    place = me % kv_group
    kv_mat = jnp.concatenate(
        [
            lax.dynamic_index_in_dim(stacked_blocks, (m - place) % kv_group, 0, keepdims=False)
            for m in range(kv_group)
        ],
        axis=0,
    )

    mask = pair_mask(tokens)
    my_rows = lambda full: lax.dynamic_slice_in_dim(full, me * rows, rows, 0)

    def summed_projections(act_list, cot):
        partials, squares = [], []
        for act in act_list:
            wide = act.astype(F32)
            scaled = (wide * gain).astype(BF)
            partials += [mm(scaled, query_mat), mm_t(scaled, kv_mat)]
            squares.append(jnp.sum(wide * wide, axis=-1, keepdims=True))
        partials.append(mm_t(cot, output_mat))
        square_mat = jnp.concatenate(squares, axis=1)
        high, low = split_f32(square_mat)
        count = len(act_list)
        filler = jnp.zeros((tokens, HD - 2 * count), BF)
        message = jnp.concatenate([p.astype(BF) for p in partials] + [high, low, filler], axis=1)
        other_half = lax.ppermute(message, "section", mirror).astype(F32)
        at = 0
        totals = []
        for p in partials:
            totals.append(p + other_half[:, at : at + p.shape[1]])
            at += p.shape[1]
        square_total = (
            square_mat + other_half[:, at : at + count] + other_half[:, at + count : at + 2 * count]
        )
        inverse = lax.rsqrt(square_total / width + EPSILON)
        out = []
        for i in range(count):
            inv = inverse[:, i : i + 1]
            out.append((totals[2 * i] * inv, totals[2 * i + 1] * inv, inv))
        return out, totals[-1].astype(BF)

    def forward_part(projected):
        queries, keyvals, _ = projected
        probs, mixed = attention(queries.astype(BF), keyvals.astype(BF), mask)
        return probs, mixed

    kv_index = [(d % 2) + 2 * (d // (shards // 2)) for d in range(shards)]
    kv_head_of = [(d % (shards // 2)) // 2 for d in range(shards)]
    my_head = me // kv_group

    def backward_part(act, projected, probs, back_mixed):
        queries, keyvals, inverse = projected
        query_back, keyval_back = attention_back(
            queries.astype(BF), keyvals.astype(BF), probs, back_mixed
        )
        back_normed = mm_t(query_back, query_mat) + mm(keyval_back, kv_mat)
        along = jnp.sum(query_back.astype(F32) * queries, axis=-1, keepdims=True) + jnp.sum(
            keyval_back.astype(F32) * keyvals, axis=-1, keepdims=True
        )
        unit = act.astype(F32) * inverse
        partial = inverse * (back_normed * gain - unit * (along / width))
        gain_part = jnp.sum(back_normed * unit, axis=0)
        normed = (unit * gain).astype(BF)
        return query_back, keyval_back, partial.astype(BF), gain_part, normed

    def scatter_sum(pieces):
        block = jnp.concatenate(pieces, axis=1)
        received = lax.all_to_all(block, "tp", split_axis=0, concat_axis=0, tiled=True)
        total = jnp.sum(received.astype(F32), axis=0)
        sizes = [p.shape[1] for p in pieces]
        at, out = 0, []
        for size in sizes:
            out.append(total[at : at + size])
            at += size
        return out

    def kv_blocks(keyval_back):
        turned_back = keyval_back.T.reshape(kv_group, -1, half)
        return jnp.stack(
            [
                jnp.where(kv_head_of[d] == my_head, turned_back[kv_index[d]], jnp.zeros((), BF))
                for d in range(shards)
            ]
        )

    act_rows, cot_rows = held[0], held[1 + ticks]
    projected, back_mixed = summed_projections([acts] + stash, cots)
    stash_projected = projected[1:]
    stash_forward = [forward_part(p) for p in stash_projected]
    forward_projected = projected[0]
    gain_total = jnp.zeros((half,), F32)
    out_rows, back_rows = [], []
    all_normed, all_query_back, all_kv_back, all_cots, all_mixed = [], [], [], [], []
    last = sections // 2 - 1
    ahead = [(i, i + 1) for i in range(last)] + [
        (sections - 1 - i, sections - 2 - i) for i in range(last)
    ]
    behind = [(b, a) for a, b in ahead]
    first_layer = (section == 0) | (section == sections - 1)
    last_layer = (section == last) | (section == last + 1)

    for k in range(ticks):
        _, mixed = forward_part(forward_projected)
        out_part = mm(mixed, output_mat).astype(BF)
        probs, kept_mixed = stash_forward[k]
        query_back, keyval_back, back_part, gain_part, normed = backward_part(
            stash[k], stash_projected[k], probs, back_mixed
        )
        gain_total = gain_total + gain_part
        pieces = [
            out_part.reshape(shards, rows, half),
            back_part.reshape(shards, rows, half),
            kv_blocks(keyval_back),
        ]
        if k + 1 == ticks:
            both = jnp.stack(split_f32(gain_total))[None]
            pieces.append(jnp.broadcast_to(both, (shards, 2, half)))
        sums = scatter_sum(pieces)
        layer_out = (act_rows.astype(F32) + sums[0]).astype(BF)
        back_input = (cot_rows.astype(F32) + sums[1]).astype(BF)
        out_rows.append(layer_out)
        back_rows.append(back_input)
        all_kv_back.append(sums[2].astype(BF).reshape(-1, tokens))
        all_normed.append(normed)
        all_query_back.append(query_back)
        all_cots.append(cots)
        all_mixed.append(kept_mixed)
        if k + 1 < ticks:
            f = layer_out.reshape(2, 2, row_count, half)
            b = back_input.reshape(2, 2, row_count, half)
            going_up = jnp.stack([f[0, 0], f[1, 1], b[1, 0], b[0, 1]])
            going_down = jnp.stack([f[1, 0], f[0, 1], b[0, 0], b[1, 1]])
            from_below = lax.ppermute(going_up, "section", ahead)
            from_above = lax.ppermute(going_down, "section", behind)
            fresh = jnp.stack(
                [fresh_acts[0, k], fresh_acts[1, k], fresh_grads[0, k], fresh_grads[1, k]]
            )
            fresh = halves(fresh)[0]
            lo = jnp.where(first_layer, fresh, from_below)
            hi = jnp.where(last_layer, going_up, from_above)
            act_rows = jnp.concatenate([lo[0], hi[1], hi[0], lo[1]], axis=0)
            cot_rows = jnp.concatenate([hi[2], lo[3], lo[2], hi[3]], axis=0)
            acts, cots = gather(jnp.stack([act_rows, cot_rows]))
            projected, back_mixed = summed_projections([acts], cots)
            forward_projected = projected[0]

    normed = jnp.concatenate(all_normed, axis=0)
    grad_query = t_mm(normed, jnp.concatenate(all_query_back, axis=0)).astype(BF)
    grad_keyval = mm(jnp.concatenate(all_kv_back, axis=1), normed).astype(BF).T
    grad_output = t_mm(
        jnp.concatenate(all_cots, axis=0), jnp.concatenate(all_mixed, axis=0)
    ).astype(BF)
    grad_gain = (sums[3][0] + sums[3][1]).astype(BF)

    leaving = jnp.stack(out_rows + back_rows).reshape(2 * ticks, 2, 2 * row_count, half)
    lo_rows, hi_rows = leaving[:, 0], leaving[:, 1]
    mine, theirs = jnp.where(lower, lo_rows, hi_rows), jnp.where(lower, hi_rows, lo_rows)
    returned = lax.ppermute(theirs, "section", mirror)
    whole = jnp.concatenate(
        [jnp.where(lower, mine, returned), jnp.where(lower, returned, mine)], axis=2
    ).reshape(2, ticks, 2, row_count, width)
    whole = whole.transpose(0, 2, 1, 3, 4)
    return (
        whole[0][None],
        whole[1][None],
        grad_query[None],
        grad_keyval[None],
        grad_output[None],
        grad_gain[None],
    )


def solution(mesh):
    in_specs = (
        P("section", None, "tp", None),
        P(None, None, "tp", None),
        P("section", None, None, "tp", None),
        P("section", None, "tp", None),
        P(None, None, "tp", None),
        P("section", None),
        P("section", None, "tp"),
        P("section", None, "tp"),
        P("section", "tp", None),
    )
    out_specs = (
        P("section", None, None, "tp", None),
        P("section", None, None, "tp", None),
        P("section", None, "tp"),
        P("section", None, "tp"),
        P("section", None, "tp"),
        P("section", None),
    )
    return jax.shard_map(
        on_device, mesh=mesh, in_specs=in_specs, out_specs=out_specs, check_vma=False
    )
```

```python
import functools
import math

import jax
import jax.numpy as jnp
from jax import lax
from jax.experimental import pallas as pl
from jax.experimental.pallas import tpu as pltpu
from jax.sharding import PartitionSpec as P

HD = 128
KVH = 4
EPSILON = 1e-05
BF = jnp.bfloat16
F32 = jnp.float32


def mm(left, right, dims=((1,), (0,))):
    return lax.dot_general(left, right, (dims, ((), ())), preferred_element_type=F32)


def mm_t(left, right):
    return mm(left, right, ((1,), (1,)))


def t_mm(left, right):
    return mm(left, right, ((0,), (0,)))


def pair_mask(tokens, row_count):
    def parts(axis):
        i = lax.broadcasted_iota(jnp.int32, (tokens, tokens), axis)
        group = (i // row_count) % 4
        return group, (i // (4 * row_count)) * row_count + i % row_count

    (query_group, query_time), (key_group, key_time) = parts(0), parts(1)
    return (query_group == key_group) & (key_time <= query_time)


def array_of(gathered_ref, index, rows):
    at = (index // 2) * 2 * rows
    block = gathered_ref[:, at : at + 2 * rows, :].astype(F32)
    part = block[:, (index % 2) * rows : (index % 2 + 1) * rows]
    return part.reshape(part.shape[0] * rows, part.shape[2])


def lane_sum(block, lanes):
    lane = lax.broadcasted_iota(jnp.int32, block.shape, 1)
    chosen = functools.reduce(jnp.logical_or, [lane == i for i in lanes])
    return jnp.sum(jnp.where(chosen, block, 0.0), axis=1, keepdims=True)


def project_body(groups, rows, gathered, gain, query_mat, kv_mat, output_mat, *outs):
    gain_row = gain[...].astype(F32)
    for index, (acts, cot) in enumerate(groups):
        message, own = outs[2 * index], outs[2 * index + 1]
        tokens = own.shape[0]
        at = 0
        squares = []
        for act in acts:
            wide = array_of(gathered, act, rows)
            scaled = (wide * gain_row).astype(BF)
            squares.append(jnp.sum(wide * wide, axis=1, keepdims=True))
            for part in (mm(scaled, query_mat[...]), mm_t(scaled, kv_mat[...])):
                own[:, at : at + part.shape[1]] = part
                message[:, at : at + part.shape[1]] = part.astype(BF)
                at += part.shape[1]
        if cot is not None:
            part = mm_t(array_of(gathered, cot, rows).astype(BF), output_mat[...])
            own[:, at : at + part.shape[1]] = part
            message[:, at : at + part.shape[1]] = part.astype(BF)
            at += part.shape[1]
        lane = lax.broadcasted_iota(jnp.int32, (tokens, HD), 1)
        kept = jnp.zeros((tokens, HD), F32)
        sent = jnp.zeros((tokens, HD), F32)
        for i, square in enumerate(squares):
            high = square.astype(BF).astype(F32)
            kept = jnp.where(lane == i, square, kept)
            sent = jnp.where(lane == i, high, sent)
            sent = jnp.where(lane == len(squares) + i, square - high, sent)
        own[:, at : at + HD] = kept
        message[:, at : at + HD] = sent.astype(BF)


def stack_heads(columns):
    return jnp.concatenate([columns[:, i : i + HD] for i in range(0, columns.shape[1], HD)], axis=0)


def unstack_heads(stacked, tokens):
    return jnp.concatenate(
        [stacked[i : i + tokens] for i in range(0, stacked.shape[0], tokens)], axis=1
    )


def softmax_of(stacked, keys, mask):
    scores = mm_t(stacked, keys) / math.sqrt(HD)
    scores = jnp.where(mask, scores, -jnp.inf)
    weights = jnp.exp(scores - jnp.max(scores, axis=1, keepdims=True))
    return weights / jnp.sum(weights, axis=1, keepdims=True)


def attend_body(
    plan, head, own_x, got_x, own_s, got_s, gathered, gain, query_mat, kv_mat, output_mat, *rest
):
    last = plan["last"]
    if last:
        gain_before, rest = rest[0], rest[1:]
    block, normed_out, query_back_out, mixed_out = rest[:4]
    rows, columns = plan["rows"], query_mat.shape[1]
    shards = block.shape[0]
    tokens, half = shards * rows, query_mat.shape[0]
    eval_columns = columns + 2 * HD
    heads = columns // HD

    def total(own, got, at, size):
        return own[:, at : at + size] + got[:, at : at + size].astype(F32)

    def projected(own, got, place, count, has_cot):
        at = count * eval_columns + (columns if has_cot else 0)
        square = lane_sum(total(own, got, at, HD), (place, count + place))
        inverse = lax.rsqrt(square / (2 * half) + EPSILON)
        start = place * eval_columns
        queries = total(own, got, start, columns) * inverse
        keyvals = total(own, got, start + columns, 2 * HD) * inverse
        return queries, keyvals, inverse

    mask = pair_mask(tokens, rows // 4)
    mask = jnp.concatenate([mask.astype(jnp.int32)] * heads, axis=0) == 1

    queries, keyvals, _ = projected(own_x, got_x, 0, plan["count_x"], True)
    keys, values = keyvals[:, :HD].astype(BF), keyvals[:, HD:].astype(BF)
    probs = softmax_of(stack_heads(queries).astype(BF), keys, mask)
    mixed = unstack_heads(mm(probs.astype(BF), values), tokens).astype(BF)
    out_part = mm(mixed, output_mat[...])

    back_mixed = total(own_x, got_x, plan["count_x"] * eval_columns, columns)
    queries, keyvals, inverse = projected(
        own_s, got_s, plan["place_s"], plan["count_s"], plan["cot_s"]
    )
    keys, values = keyvals[:, :HD].astype(BF), keyvals[:, HD:].astype(BF)
    stacked = stack_heads(queries).astype(BF)
    probs = softmax_of(stacked, keys, mask)
    mixed_out[...] = unstack_heads(mm(probs.astype(BF), values), tokens).astype(BF)
    back = stack_heads(back_mixed).astype(BF)
    back_probs = mm_t(back, values)
    inner = jnp.sum(probs * back_probs, axis=1, keepdims=True)
    back_scores = probs * (back_probs - inner) / math.sqrt(HD)
    query_back = unstack_heads(mm(back_scores.astype(BF), keys), tokens).astype(BF)
    query_back_out[...] = query_back
    key_back = mm(back_scores.T.astype(BF), stacked)
    value_back = mm(probs.T.astype(BF), back)
    keyval_wide = jnp.concatenate([key_back, value_back], axis=1)
    keyval_back = keyval_wide.astype(BF)

    back_normed = mm_t(query_back, query_mat[...]) + mm(keyval_back, kv_mat[...])
    along = jnp.sum(query_back.astype(F32) * queries, axis=1, keepdims=True) + jnp.sum(
        keyval_back.astype(F32) * keyvals, axis=1, keepdims=True
    )
    gain_row = gain[...].astype(F32)
    unit = array_of(gathered, plan["stash"], rows) * inverse
    normed_out[...] = (unit * gain_row).astype(BF)
    back_part = inverse * (back_normed * gain_row - unit * (along / (2 * half)))
    gain_part = jnp.sum(back_normed * unit, axis=0, keepdims=True)

    both = jnp.concatenate(
        [out_part.reshape(shards, rows, half), back_part.reshape(shards, rows, half)], axis=1
    )
    block[:, :, :half] = both.astype(BF)

    turned = jnp.concatenate([key_back.T, value_back.T], axis=0)
    deep = 2 * rows
    per_block = turned.shape[0] // 4
    my_head = head[0]
    pieces = []
    for k in range(4):
        piece = turned[k * per_block : (k + 1) * per_block]
        pieces.append(
            jnp.concatenate([piece[i : i + deep] for i in range(0, per_block, deep)], axis=1)
        )
    wide_lanes = pieces[0].shape[1]
    for d in range(shards):
        k = (d % 2) + 2 * (d // (shards // 2))
        kept = jnp.where(my_head == (d % (shards // 2)) // 2, pieces[k], 0.0)
        block[d, :, half : half + wide_lanes] = kept.astype(BF)

    if last:
        gain_part = gain_part + gain_before[...]
        high = gain_part.astype(BF).astype(F32)
        width = half // rows
        spread = jnp.concatenate(
            [part[:, i * width : (i + 1) * width] for part in (high, gain_part - high) for i in range(rows)],
            axis=0,
        ).astype(BF)
        for d in range(shards):
            block[d, :, half + wide_lanes :] = spread
    else:
        rest[4][...] = gain_part


VMEM = pl.BlockSpec(memory_space=pltpu.VMEM)
SMEM = pl.BlockSpec(memory_space=pltpu.SMEM)
PARAMS = pltpu.CompilerParams(vmem_limit_bytes=44 * 2**20)


def on_device(
    carried_acts,
    fresh_acts,
    stashed_acts,
    carried_grads,
    fresh_grads,
    norm_gain,
    query_weight,
    keyval_weight,
    output_weight,
):
    sections = lax.axis_size("section")
    shards = lax.axis_size("tp")
    section = lax.axis_index("section")
    me = lax.axis_index("tp")
    lower = section < sections // 2
    ticks = stashed_acts.shape[2]
    width = carried_acts.shape[3]
    half = width // 2
    row_count = carried_acts.shape[2]
    rows = 4 * row_count
    tokens = rows * shards
    query_mat, output_mat = query_weight[0], output_weight[0]
    columns = query_mat.shape[1]
    mirror = [(i, sections - 1 - i) for i in range(sections)]
    kv_group = shards // KVH

    def halves(whole):
        first, second = whole[..., :half], whole[..., half:]
        return jnp.where(lower, first, second), jnp.where(lower, second, first)

    entering = jnp.stack(
        [carried_acts[0]] + [stashed_acts[0, :, k] for k in range(ticks)] + [carried_grads[0]]
    ).reshape(ticks + 2, 2 * row_count, width)
    own, other = halves(entering)
    arrived = lax.ppermute(other, "section", mirror)
    held = jnp.concatenate(
        [jnp.where(lower, own, arrived), jnp.where(lower, arrived, own)], axis=1
    )

    kv_own = keyval_weight[0].T
    sources = [[2 * j, 2 * j + 1, shards // 2 + 2 * j, shards // 2 + 2 * j + 1] for j in range(KVH)]
    fetched = [
        lax.ppermute(
            kv_own,
            "tp",
            [
                (sources[j][(i + 2 * k) % kv_group], kv_group * j + i)
                for j in range(KVH)
                for i in range(kv_group)
            ],
        )
        for k in range(2)
    ]
    second_chip = (me // 2) % 2 == 1
    mine = jnp.stack(
        [
            jnp.where(second_chip, fetched[1], fetched[0]),
            jnp.where(second_chip, fetched[0], fetched[1]),
        ]
    )
    swapped = lax.ppermute(mine, "tp", [(i, i ^ 1) for i in range(shards)])
    even = me % 2 == 0
    kv_mat = jnp.stack(
        [jnp.where(even, mine, swapped), jnp.where(even, swapped, mine)], axis=1
    ).reshape(2 * HD, half)

    def gather(local):
        count = local.shape[0]
        spread = jnp.broadcast_to(local.reshape(1, count * rows, half), (shards, count * rows, half))
        return lax.all_to_all(spread, "tp", split_axis=0, concat_axis=0, tiled=True)

    eval_columns = columns + 2 * HD

    def project(gathered, groups):
        shapes = []
        for acts, cot in groups:
            size = len(acts) * eval_columns + (0 if cot is None else columns) + HD
            shapes += [
                jax.ShapeDtypeStruct((tokens, size), BF),
                jax.ShapeDtypeStruct((tokens, size), F32),
            ]
        outs = pl.pallas_call(
            functools.partial(project_body, groups, rows),
            out_shape=shapes,
            in_specs=[VMEM] * 5,
            out_specs=[VMEM] * len(shapes),
            compiler_params=PARAMS,
        )(gathered, norm_gain, query_mat, kv_mat, output_mat)
        return [(outs[2 * i], outs[2 * i + 1]) for i in range(len(groups))]

    def exchange(message):
        return lax.ppermute(message, "section", mirror)

    my_head = (me // kv_group).astype(jnp.int32).reshape(1)
    kv_lanes = 2 * HD // 4 // (2 * rows) * tokens

    def attend(plan, pieces, gathered, gain_before):
        last = plan["last"]
        lanes = half + kv_lanes + (half // rows if last else 0)
        shapes = [
            jax.ShapeDtypeStruct((shards, 2 * rows, lanes), BF),
            jax.ShapeDtypeStruct((tokens, half), BF),
            jax.ShapeDtypeStruct((tokens, columns), BF),
            jax.ShapeDtypeStruct((tokens, columns), BF),
        ]
        if not last:
            shapes.append(jax.ShapeDtypeStruct((1, half), F32))
        extra = [gain_before] if last else []
        return pl.pallas_call(
            functools.partial(attend_body, plan),
            out_shape=shapes,
            in_specs=[SMEM] + [VMEM] * (9 + len(extra)),
            out_specs=[VMEM] * len(shapes),
            compiler_params=PARAMS,
        )(my_head, *pieces, gathered, norm_gain, query_mat, kv_mat, output_mat, *extra)

    def reduce_blocks(block):
        received = lax.all_to_all(block, "tp", split_axis=0, concat_axis=0, tiled=True)
        return jnp.sum(received.astype(F32), axis=0)

    def kv_rows(total):
        part = total[:, half : half + kv_lanes]
        return jnp.concatenate(
            [part[:, i : i + tokens] for i in range(0, kv_lanes, tokens)], axis=0
        ).astype(BF)

    def all_tokens(gathered, index):
        return gathered[:, index * rows : (index + 1) * rows].reshape(tokens, half)

    last = sections // 2 - 1
    ahead = [(i, i + 1) for i in range(last)] + [
        (sections - 1 - i, sections - 2 - i) for i in range(last)
    ]
    behind = [(b, a) for a, b in ahead]
    first_layer = (section == 0) | (section == sections - 1)
    last_layer = (section == last) | (section == last + 1)

    gathered = gather(held)
    kept = gathered
    cot_index = ticks + 1
    all_cots = [all_tokens(gathered, cot_index)]
    projected = project(gathered, [((0, 1), cot_index)] + [((k,), None) for k in range(2, 1 + ticks)])
    (message, own_x), later = projected[0], projected[1:]
    got_x = exchange(message)
    own_s, got_s = own_x, got_x
    act_rows, cot_rows = held[0], held[cot_index]
    gain_total = None
    out_rows, back_rows = [], []
    all_normed, all_query_back, all_kv_back, all_mixed = [], [], [], []
    for k in range(ticks):
        plan = {
            "last": k + 1 == ticks,
            "rows": rows,
            "count_x": 2 if k == 0 else 1,
            "place_s": 1 if k == 0 else 0,
            "count_s": 2 if k == 0 else 1,
            "cot_s": k == 0,
            "stash": 1 + k,
        }
        block, normed, query_back, mixed, *rest = attend(
            plan, (own_x, got_x, own_s, got_s), kept, gain_total
        )
        if k + 1 < ticks:
            gain_total = rest[0] if gain_total is None else gain_total + rest[0]
            block, message_s = lax.optimization_barrier((block, later[k][0]))
            own_s, got_s = later[k][1], exchange(message_s)
        total = reduce_blocks(block)
        layer_out = (act_rows.astype(F32) + total[:rows, :half]).astype(BF)
        back_input = (cot_rows.astype(F32) + total[rows:, :half]).astype(BF)
        out_rows.append(layer_out)
        back_rows.append(back_input)
        all_kv_back.append(kv_rows(total))
        all_normed.append(normed)
        all_query_back.append(query_back)
        all_mixed.append(mixed)
        if k + 1 < ticks:
            f = layer_out.reshape(2, 2, row_count, half)
            b = back_input.reshape(2, 2, row_count, half)
            going_up = jnp.stack([f[0, 0], f[1, 1], b[1, 0], b[0, 1]])
            going_down = jnp.stack([f[1, 0], f[0, 1], b[0, 0], b[1, 1]])
            going_up, going_down = lax.optimization_barrier((going_up, going_down))
            from_below = lax.ppermute(going_up, "section", ahead)
            from_above = lax.ppermute(going_down, "section", behind)
            from_below, from_above = lax.optimization_barrier((from_below, from_above))
            fresh = jnp.stack(
                [fresh_acts[0, k], fresh_acts[1, k], fresh_grads[0, k], fresh_grads[1, k]]
            )
            fresh = halves(fresh)[0]
            lo = jnp.where(first_layer, fresh, from_below)
            hi = jnp.where(last_layer, going_up, from_above)
            act_rows = jnp.concatenate([lo[0], hi[1], hi[0], lo[1]], axis=0)
            cot_rows = jnp.concatenate([hi[2], lo[3], lo[2], hi[3]], axis=0)
            gathered = gather(jnp.stack([act_rows, cot_rows]))
            all_cots.append(all_tokens(gathered, 1))
            ((message, own_x),) = project(gathered, [((0,), 1)])
            got_x = exchange(message)

    normed = jnp.concatenate(all_normed, axis=0)
    grad_query = t_mm(normed, jnp.concatenate(all_query_back, axis=0)).astype(BF)
    grad_keyval = mm(jnp.concatenate(all_kv_back, axis=1), normed).astype(BF).T
    grad_output = t_mm(
        jnp.concatenate(all_cots, axis=0), jnp.concatenate(all_mixed, axis=0)
    ).astype(BF)
    gain_lanes = total[:, half + kv_lanes :]
    grad_gain = (gain_lanes[:rows] + gain_lanes[rows:]).astype(BF).reshape(half)

    leaving = jnp.stack(out_rows + back_rows).reshape(2 * ticks, 2, 2 * row_count, half)
    lo_rows, hi_rows = leaving[:, 0], leaving[:, 1]
    mine, theirs = jnp.where(lower, lo_rows, hi_rows), jnp.where(lower, hi_rows, lo_rows)
    returned = lax.ppermute(theirs, "section", mirror)
    whole = jnp.concatenate(
        [jnp.where(lower, mine, returned), jnp.where(lower, returned, mine)], axis=2
    ).reshape(2, ticks, 2, row_count, width)
    whole = whole.transpose(0, 2, 1, 3, 4)
    return (
        whole[0][None],
        whole[1][None],
        grad_query[None],
        grad_keyval[None],
        grad_output[None],
        grad_gain[None],
    )


def solution(mesh):
    in_specs = (
        P("section", None, "tp", None),
        P(None, None, "tp", None),
        P("section", None, None, "tp", None),
        P("section", None, "tp", None),
        P(None, None, "tp", None),
        P("section", None),
        P("section", None, "tp"),
        P("section", None, "tp"),
        P("section", "tp", None),
    )
    out_specs = (
        P("section", None, None, "tp", None),
        P("section", None, None, "tp", None),
        P("section", None, "tp"),
        P("section", None, "tp"),
        P("section", None, "tp"),
        P("section", None),
    )
    return jax.shard_map(
        on_device, mesh=mesh, in_specs=in_specs, out_specs=out_specs, check_vma=False
    )
```

```python
import functools
import math

import jax
import jax.numpy as jnp
from jax import lax
from jax.experimental import pallas as pl
from jax.experimental.pallas import tpu as pltpu
from jax.sharding import PartitionSpec as P

HD = 128
KVH = 4
EPSILON = 1e-05
BF = jnp.bfloat16
F32 = jnp.float32


def mm(left, right, dims=((1,), (0,))):
    return lax.dot_general(left, right, (dims, ((), ())), preferred_element_type=F32)


def mm_t(left, right):
    return mm(left, right, ((1,), (1,)))


def t_mm(left, right):
    return mm(left, right, ((0,), (0,)))


def pair_mask(tokens, row_count):
    def parts(axis):
        i = lax.broadcasted_iota(jnp.int32, (tokens, tokens), axis)
        group = (i // row_count) % 4
        return group, (i // (4 * row_count)) * row_count + i % row_count

    (query_group, query_time), (key_group, key_time) = parts(0), parts(1)
    return (query_group == key_group) & (key_time <= query_time)


def array_of(gathered_ref, index, rows):
    part = gathered_ref[...].astype(F32)[:, index * rows : (index + 1) * rows]
    return part.reshape(part.shape[0] * rows, part.shape[2])


def lane_sum(block, lanes):
    lane = lax.broadcasted_iota(jnp.int32, block.shape, 1)
    chosen = functools.reduce(jnp.logical_or, [lane == i for i in lanes])
    return jnp.sum(jnp.where(chosen, block, 0.0), axis=1, keepdims=True)


def project_body(groups, rows, gathered, gain, query_mat, kv_mat, output_mat, *outs):
    gain_row = gain[...].astype(F32)
    for index, (acts, cot) in enumerate(groups):
        message, own = outs[2 * index], outs[2 * index + 1]
        tokens = own.shape[0]
        at = 0
        squares = []
        for act in acts:
            wide = array_of(gathered, act, rows)
            scaled = (wide * gain_row).astype(BF)
            squares.append(jnp.sum(wide * wide, axis=1, keepdims=True))
            for part in (mm(scaled, query_mat[...]), mm_t(scaled, kv_mat[...])):
                own[:, at : at + part.shape[1]] = part
                message[:, at : at + part.shape[1]] = part.astype(BF)
                at += part.shape[1]
        if cot is not None:
            part = mm_t(array_of(gathered, cot, rows).astype(BF), output_mat[...])
            own[:, at : at + part.shape[1]] = part
            message[:, at : at + part.shape[1]] = part.astype(BF)
            at += part.shape[1]
        lane = lax.broadcasted_iota(jnp.int32, (tokens, HD), 1)
        kept = jnp.zeros((tokens, HD), F32)
        sent = jnp.zeros((tokens, HD), F32)
        for i, square in enumerate(squares):
            high = square.astype(BF).astype(F32)
            kept = jnp.where(lane == i, square, kept)
            sent = jnp.where(lane == i, high, sent)
            sent = jnp.where(lane == len(squares) + i, square - high, sent)
        own[:, at : at + HD] = kept
        message[:, at : at + HD] = sent.astype(BF)


def stack_heads(columns):
    return jnp.concatenate([columns[:, i : i + HD] for i in range(0, columns.shape[1], HD)], axis=0)


def unstack_heads(stacked, tokens):
    return jnp.concatenate(
        [stacked[i : i + tokens] for i in range(0, stacked.shape[0], tokens)], axis=1
    )


def softmax_of(stacked, keys, mask):
    scores = mm_t(stacked, keys) / math.sqrt(HD)
    scores = jnp.where(mask, scores, -jnp.inf)
    weights = jnp.exp(scores - jnp.max(scores, axis=1, keepdims=True))
    return weights / jnp.sum(weights, axis=1, keepdims=True)


def attend_body(
    plan, own_x, got_x, own_s, got_s, gathered, gain, query_mat, kv_mat, output_mat, *rest
):
    last = plan["last"]
    if last:
        gain_before, rest = rest[0], rest[1:]
    block, normed_out, query_back_out, mixed_out, keyval_back_out = rest[:5]
    rows, columns = plan["rows"], query_mat.shape[1]
    shards = block.shape[0]
    tokens, half = shards * rows, query_mat.shape[0]
    eval_columns = columns + 2 * HD
    heads = columns // HD

    def total(own, got, at, size):
        return own[:, at : at + size] + got[:, at : at + size].astype(F32)

    def projected(own, got, place, count, has_cot):
        at = count * eval_columns + (columns if has_cot else 0)
        square = lane_sum(total(own, got, at, HD), (place, count + place))
        inverse = lax.rsqrt(square / (2 * half) + EPSILON)
        start = place * eval_columns
        queries = total(own, got, start, columns) * inverse
        keyvals = total(own, got, start + columns, 2 * HD) * inverse
        return queries, keyvals, inverse

    mask = pair_mask(tokens, rows // 4)
    mask = jnp.concatenate([mask.astype(jnp.int32)] * heads, axis=0) == 1

    queries, keyvals, _ = projected(own_x, got_x, 0, plan["count_x"], True)
    keys, values = keyvals[:, :HD].astype(BF), keyvals[:, HD:].astype(BF)
    probs = softmax_of(stack_heads(queries).astype(BF), keys, mask)
    mixed = unstack_heads(mm(probs.astype(BF), values), tokens).astype(BF)
    out_part = mm(mixed, output_mat[...])

    back_mixed = total(own_x, got_x, plan["count_x"] * eval_columns, columns)
    queries, keyvals, inverse = projected(
        own_s, got_s, plan["place_s"], plan["count_s"], plan["cot_s"]
    )
    keys, values = keyvals[:, :HD].astype(BF), keyvals[:, HD:].astype(BF)
    stacked = stack_heads(queries).astype(BF)
    probs = softmax_of(stacked, keys, mask)
    mixed_out[...] = unstack_heads(mm(probs.astype(BF), values), tokens).astype(BF)
    back = stack_heads(back_mixed).astype(BF)
    back_probs = mm_t(back, values)
    inner = jnp.sum(probs * back_probs, axis=1, keepdims=True)
    back_scores = probs * (back_probs - inner) / math.sqrt(HD)
    query_back = unstack_heads(mm(back_scores.astype(BF), keys), tokens).astype(BF)
    query_back_out[...] = query_back
    key_back = mm(back_scores.T.astype(BF), stacked)
    value_back = mm(probs.T.astype(BF), back)
    keyval_back = jnp.concatenate([key_back, value_back], axis=1).astype(BF)

    back_normed = mm_t(query_back, query_mat[...]) + mm(keyval_back, kv_mat[...])
    along = jnp.sum(query_back.astype(F32) * queries, axis=1, keepdims=True) + jnp.sum(
        keyval_back.astype(F32) * keyvals, axis=1, keepdims=True
    )
    gain_row = gain[...].astype(F32)
    unit = array_of(gathered, plan["stash"], rows) * inverse
    normed_out[...] = (unit * gain_row).astype(BF)
    back_part = inverse * (back_normed * gain_row - unit * (along / (2 * half)))
    gain_part = jnp.sum(back_normed * unit, axis=0, keepdims=True)

    both = jnp.concatenate(
        [out_part.reshape(shards, rows, half), back_part.reshape(shards, rows, half)], axis=1
    )
    block[:, :, :half] = both.astype(BF)

    keyval_back_out[...] = jnp.concatenate([key_back.T, value_back.T], axis=0).astype(BF)

    if last:
        gain_part = gain_part + gain_before[...]
        high = gain_part.astype(BF).astype(F32)
        width = half // rows
        spread = jnp.concatenate(
            [part[:, i * width : (i + 1) * width] for part in (high, gain_part - high) for i in range(rows)],
            axis=0,
        ).astype(BF)
        for d in range(shards):
            block[d, :, half:] = spread
    else:
        rest[5][...] = gain_part


VMEM = pl.BlockSpec(memory_space=pltpu.VMEM)
PARAMS = pltpu.CompilerParams(vmem_limit_bytes=24 * 2**20)


def on_device(
    carried_acts,
    fresh_acts,
    stashed_acts,
    carried_grads,
    fresh_grads,
    norm_gain,
    query_weight,
    keyval_weight,
    output_weight,
):
    sections = lax.axis_size("section")
    shards = lax.axis_size("tp")
    section = lax.axis_index("section")
    me = lax.axis_index("tp")
    lower = section < sections // 2
    ticks = stashed_acts.shape[2]
    width = carried_acts.shape[3]
    half = width // 2
    row_count = carried_acts.shape[2]
    rows = 4 * row_count
    tokens = rows * shards
    query_mat, output_mat = query_weight[0], output_weight[0]
    columns = query_mat.shape[1]
    mirror = [(i, sections - 1 - i) for i in range(sections)]
    kv_group = shards // KVH

    def halves(whole):
        first, second = whole[..., :half], whole[..., half:]
        return jnp.where(lower, first, second), jnp.where(lower, second, first)

    entering = jnp.stack(
        [carried_acts[0], carried_grads[0]] + [stashed_acts[0, :, k] for k in range(ticks)]
    ).reshape(ticks + 2, 2 * row_count, width)
    own, other = halves(entering)
    arrived = lax.ppermute(other, "section", mirror)
    held = jnp.concatenate(
        [jnp.where(lower, own, arrived), jnp.where(lower, arrived, own)], axis=1
    )

    kv_own = keyval_weight[0].T
    sources = [[2 * j, 2 * j + 1, shards // 2 + 2 * j, shards // 2 + 2 * j + 1] for j in range(KVH)]
    kv_routes = [
        [
            (sources[j][(i + 2 * k) % kv_group], kv_group * j + i)
            for j in range(KVH)
            for i in range(kv_group)
        ]
        for k in range(2)
    ]
    swap_cores = [(i, i ^ 1) for i in range(shards)]
    fetched = [lax.ppermute(kv_own, "tp", route) for route in kv_routes]
    held, fetched = lax.optimization_barrier((held, fetched))
    second_chip = (me // 2) % 2 == 1
    mine = jnp.stack(
        [
            jnp.where(second_chip, fetched[1], fetched[0]),
            jnp.where(second_chip, fetched[0], fetched[1]),
        ]
    )
    swapped = lax.ppermute(mine, "tp", swap_cores)
    even = me % 2 == 0
    kv_mat = jnp.stack(
        [jnp.where(even, mine, swapped), jnp.where(even, swapped, mine)], axis=1
    ).reshape(2 * HD, half)

    def gather(local):
        count = local.shape[0]
        spread = jnp.broadcast_to(local.reshape(1, count * rows, half), (shards, count * rows, half))
        return lax.all_to_all(spread, "tp", split_axis=0, concat_axis=0, tiled=True)

    eval_columns = columns + 2 * HD

    def project(gathered, groups):
        shapes = []
        for acts, cot in groups:
            size = len(acts) * eval_columns + (0 if cot is None else columns) + HD
            shapes += [
                jax.ShapeDtypeStruct((tokens, size), BF),
                jax.ShapeDtypeStruct((tokens, size), F32),
            ]
        outs = pl.pallas_call(
            functools.partial(project_body, groups, rows),
            out_shape=shapes,
            in_specs=[VMEM] * 5,
            out_specs=[VMEM] * len(shapes),
            compiler_params=PARAMS,
        )(gathered, norm_gain, query_mat, kv_mat, output_mat)
        return [(outs[2 * i], outs[2 * i + 1]) for i in range(len(groups))]

    def exchange(message):
        return lax.ppermute(message, "section", mirror)

    def attend(plan, pieces, gathered, gain_before):
        last = plan["last"]
        lanes = half + (half // rows if last else 0)
        shapes = [
            jax.ShapeDtypeStruct((shards, 2 * rows, lanes), BF),
            jax.ShapeDtypeStruct((tokens, half), BF),
            jax.ShapeDtypeStruct((tokens, columns), BF),
            jax.ShapeDtypeStruct((tokens, columns), BF),
            jax.ShapeDtypeStruct((2 * HD, tokens), BF),
        ]
        if not last:
            shapes.append(jax.ShapeDtypeStruct((1, half), F32))
        extra = [gain_before] if last else []
        return pl.pallas_call(
            functools.partial(attend_body, plan),
            out_shape=shapes,
            in_specs=[VMEM] * (9 + len(extra)),
            out_specs=[VMEM] * len(shapes),
            compiler_params=PARAMS,
        )(*pieces, gathered, norm_gain, query_mat, kv_mat, output_mat, *extra)

    def reduce_blocks(block):
        received = lax.all_to_all(block, "tp", split_axis=0, concat_axis=0, tiled=True)
        return jnp.sum(received.astype(F32), axis=0)

    def reduce_kv(blocks):
        parts = blocks.reshape(2, 2, HD // 2, -1)
        low, high = parts[:, 0], parts[:, 1]
        got = lax.ppermute(jnp.where(even, high, low), "tp", swap_cores)
        chip = (jnp.where(even, low, high).astype(F32) + got.astype(F32)).astype(BF)
        sends = (
            jnp.where(second_chip, chip[1], chip[0]),
            jnp.where(second_chip, chip[0], chip[1]),
        )
        arrived = [
            lax.ppermute(send, "tp", [(b, a) for a, b in route])
            for send, route in zip(sends, kv_routes)
        ]
        return (arrived[0].astype(F32) + arrived[1].astype(F32)).astype(BF)

    def all_tokens(gathered, index):
        return gathered[:, index * rows : (index + 1) * rows].reshape(tokens, half)

    last = sections // 2 - 1
    ahead = [(i, i + 1) for i in range(last)] + [
        (sections - 1 - i, sections - 2 - i) for i in range(last)
    ]
    behind = [(b, a) for a, b in ahead]
    first_layer = (section == 0) | (section == sections - 1)
    last_layer = (section == last) | (section == last + 1)

    gathered = gather(held[:3])
    all_cots = [all_tokens(gathered, 1)]
    ((message, own_x),) = project(gathered, [((0, 2), 1)])
    message, later_rows = lax.optimization_barrier((message, held[3:]))
    got_x = exchange(message)
    later = gather(later_rows)
    got_x, later = lax.optimization_barrier((got_x, later))
    later_projected = project(later, [((i,), None) for i in range(ticks - 1)])
    own_s, got_s = own_x, got_x
    act_rows, cot_rows = held[0], held[1]
    gain_total = None
    out_rows, back_rows = [], []
    all_normed, all_query_back, all_kv_back, all_mixed = [], [], [], []
    for k in range(ticks):
        first = k == 0
        plan = {
            "last": k + 1 == ticks,
            "rows": rows,
            "count_x": 2 if first else 1,
            "place_s": 1 if first else 0,
            "count_s": 2 if first else 1,
            "cot_s": first,
            "stash": 2 if first else k - 1,
        }
        block, normed, query_back, mixed, kv_back, *rest = attend(
            plan, (own_x, got_x, own_s, got_s), gathered if first else later, gain_total
        )
        if k + 1 < ticks:
            gain_total = rest[0] if gain_total is None else gain_total + rest[0]
        total = reduce_blocks(block)
        layer_out = (act_rows.astype(F32) + total[:rows, :half]).astype(BF)
        back_input = (cot_rows.astype(F32) + total[rows:, :half]).astype(BF)
        out_rows.append(layer_out)
        back_rows.append(back_input)
        all_kv_back.append(kv_back)
        all_normed.append(normed)
        all_query_back.append(query_back)
        all_mixed.append(mixed)
        if k + 1 < ticks:
            f = layer_out.reshape(2, 2, row_count, half)
            b = back_input.reshape(2, 2, row_count, half)
            going_up = jnp.stack([f[0, 0], f[1, 1], b[1, 0], b[0, 1]])
            going_down = jnp.stack([f[1, 0], f[0, 1], b[0, 0], b[1, 1]])
            going_up, going_down = lax.optimization_barrier((going_up, going_down))
            from_below = lax.ppermute(going_up, "section", ahead)
            from_above = lax.ppermute(going_down, "section", behind)
            from_below, from_above = lax.optimization_barrier((from_below, from_above))
            fresh = jnp.stack(
                [fresh_acts[0, k], fresh_acts[1, k], fresh_grads[0, k], fresh_grads[1, k]]
            )
            fresh = halves(fresh)[0]
            lo = jnp.where(first_layer, fresh, from_below)
            hi = jnp.where(last_layer, going_up, from_above)
            act_rows = jnp.concatenate([lo[0], hi[1], hi[0], lo[1]], axis=0)
            cot_rows = jnp.concatenate([hi[2], lo[3], lo[2], hi[3]], axis=0)
            entering = jnp.stack([act_rows, cot_rows])
            entering, message_s = lax.optimization_barrier((entering, later_projected[k][0]))
            own_s, got_s = later_projected[k][1], exchange(message_s)
            moved = gather(entering)
            moved, got_s = lax.optimization_barrier((moved, got_s))
            all_cots.append(all_tokens(moved, 1))
            ((message, own_x),) = project(moved, [((0,), 1)])
            got_x = exchange(message)

    normed = jnp.concatenate(all_normed, axis=0)
    grad_query = t_mm(normed, jnp.concatenate(all_query_back, axis=0)).astype(BF)
    grad_keyval = mm(reduce_kv(jnp.concatenate(all_kv_back, axis=1)), normed).astype(BF).T
    grad_output = t_mm(
        jnp.concatenate(all_cots, axis=0), jnp.concatenate(all_mixed, axis=0)
    ).astype(BF)
    gain_lanes = total[:, half:]
    grad_gain = (gain_lanes[:rows] + gain_lanes[rows:]).astype(BF).reshape(half)

    leaving = jnp.stack(out_rows + back_rows).reshape(2 * ticks, 2, 2 * row_count, half)
    lo_rows, hi_rows = leaving[:, 0], leaving[:, 1]
    mine, theirs = jnp.where(lower, lo_rows, hi_rows), jnp.where(lower, hi_rows, lo_rows)
    returned = lax.ppermute(theirs, "section", mirror)
    whole = jnp.concatenate(
        [jnp.where(lower, mine, returned), jnp.where(lower, returned, mine)], axis=2
    ).reshape(2, ticks, 2, row_count, width)
    whole = whole.transpose(0, 2, 1, 3, 4)
    return (
        whole[0][None],
        whole[1][None],
        grad_query[None],
        grad_keyval[None],
        grad_output[None],
        grad_gain[None],
    )


def solution(mesh):
    in_specs = (
        P("section", None, "tp", None),
        P(None, None, "tp", None),
        P("section", None, None, "tp", None),
        P("section", None, "tp", None),
        P(None, None, "tp", None),
        P("section", None),
        P("section", None, "tp"),
        P("section", None, "tp"),
        P("section", "tp", None),
    )
    out_specs = (
        P("section", None, None, "tp", None),
        P("section", None, None, "tp", None),
        P("section", None, "tp"),
        P("section", None, "tp"),
        P("section", None, "tp"),
        P("section", None),
    )
    return jax.shard_map(
        on_device, mesh=mesh, in_specs=in_specs, out_specs=out_specs, check_vma=False
    )
```

```python
import functools
import math

import jax
import jax.numpy as jnp
from jax import lax
from jax.experimental import pallas as pl
from jax.experimental.pallas import tpu as pltpu
from jax.sharding import PartitionSpec as P

HD = 128
KVH = 4
EPSILON = 1e-05
BF = jnp.bfloat16
F32 = jnp.float32


def mm(left, right, dims=((1,), (0,))):
    return lax.dot_general(left, right, (dims, ((), ())), preferred_element_type=F32)


def mm_t(left, right):
    return mm(left, right, ((1,), (1,)))


def t_mm(left, right):
    return mm(left, right, ((0,), (0,)))


def pair_mask(tokens, row_count):
    def parts(axis):
        i = lax.broadcasted_iota(jnp.int32, (tokens, tokens), axis)
        group = (i // row_count) % 4
        return group, (i // (4 * row_count)) * row_count + i % row_count

    (query_group, query_time), (key_group, key_time) = parts(0), parts(1)
    return (query_group == key_group) & (key_time <= query_time)


def array_of(gathered_ref, index, rows):
    part = gathered_ref[...].astype(F32)[:, index * rows : (index + 1) * rows]
    return part.reshape(part.shape[0] * rows, part.shape[2])


def lane_sum(block, lanes):
    lane = lax.broadcasted_iota(jnp.int32, block.shape, 1)
    chosen = functools.reduce(jnp.logical_or, [lane == i for i in lanes])
    return jnp.sum(jnp.where(chosen, block, 0.0), axis=1, keepdims=True)


def project_body(groups, kept_arrays, far, rows, gathered, gain, query_mat, kv_mat, output_mat, *rest):
    results, buffers, sems = rest[: len(far)], rest[len(far) : -1], rest[-1]
    places = [i for i, is_far in enumerate(far) if is_far]
    outs = [buffers[places.index(i)] if is_far else results[i] for i, is_far in enumerate(far)]
    copies = []

    def send(index):
        if far[index]:
            place = places.index(index)
            copies.append(pltpu.make_async_copy(buffers[place], results[index], sems.at[place]))
            copies[-1].start()

    for i, kept_array in enumerate(kept_arrays):
        index = 2 * len(groups) + i
        outs[index][...] = array_of(gathered, kept_array, rows).astype(BF)
        send(index)
    gain_row = gain[...].astype(F32)
    for index, (acts, cot) in enumerate(groups):
        message, own = outs[2 * index], outs[2 * index + 1]
        tokens = own.shape[0]
        at = 0
        squares = []
        for act in acts:
            wide = array_of(gathered, act, rows)
            scaled = (wide * gain_row).astype(BF)
            squares.append(jnp.sum(wide * wide, axis=1, keepdims=True))
            for part in (mm(scaled, query_mat[...]), mm_t(scaled, kv_mat[...])):
                own[:, at : at + part.shape[1]] = part
                message[:, at : at + part.shape[1]] = part.astype(BF)
                at += part.shape[1]
        if cot is not None:
            part = mm_t(array_of(gathered, cot, rows).astype(BF), output_mat[...])
            own[:, at : at + part.shape[1]] = part
            message[:, at : at + part.shape[1]] = part.astype(BF)
            at += part.shape[1]
        lane = lax.broadcasted_iota(jnp.int32, (tokens, HD), 1)
        kept = jnp.zeros((tokens, HD), F32)
        sent = jnp.zeros((tokens, HD), F32)
        for i, square in enumerate(squares):
            high = square.astype(BF).astype(F32)
            kept = jnp.where(lane == i, square, kept)
            sent = jnp.where(lane == i, high, sent)
            sent = jnp.where(lane == len(squares) + i, square - high, sent)
        own[:, at : at + HD] = kept
        message[:, at : at + HD] = sent.astype(BF)
        send(2 * index)
        send(2 * index + 1)
    for copy in copies:
        copy.wait()


def stack_heads(columns):
    return jnp.concatenate([columns[:, i : i + HD] for i in range(0, columns.shape[1], HD)], axis=0)


def unstack_heads(stacked, tokens):
    return jnp.concatenate(
        [stacked[i : i + tokens] for i in range(0, stacked.shape[0], tokens)], axis=1
    )


def softmax_of(stacked, keys, mask):
    scores = mm_t(stacked, keys) / math.sqrt(HD)
    scores = jnp.where(mask, scores, -jnp.inf)
    weights = jnp.exp(scores - jnp.max(scores, axis=1, keepdims=True))
    return weights / jnp.sum(weights, axis=1, keepdims=True)


def attend_body(
    plan, pieces, own_x, got_x, *rest
):
    last = plan["last"]
    own_s, got_s = (own_x, got_x) if pieces == 2 else rest[: pieces - 2]
    stash, gain, query_mat, kv_mat, output_mat, *rest = rest[pieces - 2 :]
    if last:
        gain_before, rest = rest[0], rest[1:]
    outs, block, sems = rest[: plan["outs"]], rest[plan["outs"]], rest[-1]
    leaving = []

    def leave(index, value):
        buffer = rest[plan["outs"] + index]
        buffer[...] = value
        send(index)

    def send(index):
        copy = pltpu.make_async_copy(
            rest[plan["outs"] + index], outs[index], sems.at[index]
        )
        copy.start()
        leaving.append(copy)
    rows, columns = plan["rows"], query_mat.shape[1]
    shards = block.shape[0]
    tokens, half = shards * rows, query_mat.shape[0]
    eval_columns = columns + 2 * HD
    heads = columns // HD

    def total(own, got, at, size):
        return own[:, at : at + size] + got[:, at : at + size].astype(F32)

    def projected(own, got, place, count, has_cot):
        at = count * eval_columns + (columns if has_cot else 0)
        square = lane_sum(total(own, got, at, HD), (place, count + place))
        inverse = lax.rsqrt(square / (2 * half) + EPSILON)
        start = place * eval_columns
        queries = total(own, got, start, columns) * inverse
        keyvals = total(own, got, start + columns, 2 * HD) * inverse
        return queries, keyvals, inverse

    mask = pair_mask(tokens, rows // 4)
    mask = jnp.concatenate([mask.astype(jnp.int32)] * heads, axis=0) == 1

    queries, keyvals, _ = projected(own_x, got_x, 0, plan["count_x"], True)
    keys, values = keyvals[:, :HD].astype(BF), keyvals[:, HD:].astype(BF)
    probs = softmax_of(stack_heads(queries).astype(BF), keys, mask)
    mixed = unstack_heads(mm(probs.astype(BF), values), tokens).astype(BF)
    out_part = mm(mixed, output_mat[...])

    back_mixed = total(own_x, got_x, plan["count_x"] * eval_columns, columns)
    queries, keyvals, inverse = projected(
        own_s, got_s, plan["place_s"], plan["count_s"], plan["cot_s"]
    )
    keys, values = keyvals[:, :HD].astype(BF), keyvals[:, HD:].astype(BF)
    stacked = stack_heads(queries).astype(BF)
    probs = softmax_of(stacked, keys, mask)
    leave(3, unstack_heads(mm(probs.astype(BF), values), tokens).astype(BF))
    back = stack_heads(back_mixed).astype(BF)
    back_probs = mm_t(back, values)
    inner = jnp.sum(probs * back_probs, axis=1, keepdims=True)
    back_scores = probs * (back_probs - inner) / math.sqrt(HD)
    query_back = unstack_heads(mm(back_scores.astype(BF), keys), tokens).astype(BF)
    leave(2, query_back)
    key_back = mm(back_scores.T.astype(BF), stacked)
    value_back = mm(probs.T.astype(BF), back)
    keyval_back = jnp.concatenate([key_back, value_back], axis=1).astype(BF)
    leave(4, jnp.concatenate([key_back.T, value_back.T], axis=0).astype(BF))

    back_normed = mm_t(query_back, query_mat[...]) + mm(keyval_back, kv_mat[...])
    along = jnp.sum(query_back.astype(F32) * queries, axis=1, keepdims=True) + jnp.sum(
        keyval_back.astype(F32) * keyvals, axis=1, keepdims=True
    )
    gain_row = gain[...].astype(F32)
    unit = stash[...].astype(F32) * inverse
    leave(1, (unit * gain_row).astype(BF))
    back_part = inverse * (back_normed * gain_row - unit * (along / (2 * half)))
    gain_part = jnp.sum(back_normed * unit, axis=0, keepdims=True)

    both = jnp.concatenate(
        [out_part.reshape(shards, rows, half), back_part.reshape(shards, rows, half)], axis=1
    )
    block[:, :, :half] = both.astype(BF)

    if last:
        gain_part = gain_part + gain_before[...]
        high = gain_part.astype(BF).astype(F32)
        width = half // rows
        spread = jnp.concatenate(
            [part[:, i * width : (i + 1) * width] for part in (high, gain_part - high) for i in range(rows)],
            axis=0,
        ).astype(BF)
        for d in range(shards):
            block[d, :, half:] = spread
    else:
        leave(5, gain_part)
    send(0)
    for copy in leaving:
        copy.wait()


VMEM = pl.BlockSpec(memory_space=pltpu.VMEM)
HBM = pl.BlockSpec(memory_space=pltpu.HBM)
PARAMS = pltpu.CompilerParams(vmem_limit_bytes=24 * 2**20)


def on_device(
    carried_acts,
    fresh_acts,
    stashed_acts,
    carried_grads,
    fresh_grads,
    norm_gain,
    query_weight,
    keyval_weight,
    output_weight,
):
    sections = lax.axis_size("section")
    shards = lax.axis_size("tp")
    section = lax.axis_index("section")
    me = lax.axis_index("tp")
    lower = section < sections // 2
    ticks = stashed_acts.shape[2]
    width = carried_acts.shape[3]
    half = width // 2
    row_count = carried_acts.shape[2]
    rows = 4 * row_count
    tokens = rows * shards
    query_mat, output_mat = query_weight[0], output_weight[0]
    columns = query_mat.shape[1]
    mirror = [(i, sections - 1 - i) for i in range(sections)]
    kv_group = shards // KVH

    def halves(whole):
        first, second = whole[..., :half], whole[..., half:]
        return jnp.where(lower, first, second), jnp.where(lower, second, first)

    entering = jnp.stack(
        [carried_acts[0], carried_grads[0]] + [stashed_acts[0, :, k] for k in range(ticks)]
    ).reshape(ticks + 2, 2 * row_count, width)
    own, other = halves(entering)
    arrived = lax.ppermute(other, "section", mirror)
    held = jnp.concatenate(
        [jnp.where(lower, own, arrived), jnp.where(lower, arrived, own)], axis=1
    )

    kv_own = keyval_weight[0].T
    sources = [[2 * j, 2 * j + 1, shards // 2 + 2 * j, shards // 2 + 2 * j + 1] for j in range(KVH)]
    kv_routes = [
        [
            (sources[j][(i + 2 * k) % kv_group], kv_group * j + i)
            for j in range(KVH)
            for i in range(kv_group)
        ]
        for k in range(2)
    ]
    swap_cores = [(i, i ^ 1) for i in range(shards)]
    fetched = [lax.ppermute(kv_own, "tp", route) for route in kv_routes]
    held, fetched = lax.optimization_barrier((held, fetched))
    second_chip = (me // 2) % 2 == 1
    mine = jnp.stack(
        [
            jnp.where(second_chip, fetched[1], fetched[0]),
            jnp.where(second_chip, fetched[0], fetched[1]),
        ]
    )
    swapped = lax.ppermute(mine, "tp", swap_cores)
    even = me % 2 == 0
    kv_mat = jnp.stack(
        [jnp.where(even, mine, swapped), jnp.where(even, swapped, mine)], axis=1
    ).reshape(2 * HD, half)

    def gather(local):
        count = local.shape[0]
        spread = jnp.broadcast_to(local.reshape(1, count * rows, half), (shards, count * rows, half))
        return lax.all_to_all(spread, "tp", split_axis=0, concat_axis=0, tiled=True)

    def gather_two_level(local):
        count, chips = local.shape[0], shards // 2
        spread = jnp.broadcast_to(local.reshape(1, count * rows, half), (chips, count * rows, half))
        groups = [[2 * chip + core for chip in range(chips)] for core in range(2)]
        mine = lax.all_to_all(
            spread, "tp", split_axis=0, concat_axis=0, axis_index_groups=groups, tiled=True
        )
        other = lax.ppermute(mine, "tp", swap_cores)
        both = jnp.stack(
            [jnp.where(even, mine, other), jnp.where(even, other, mine)], axis=1
        )
        return both.reshape(shards, count * rows, half)

    eval_columns = columns + 2 * HD

    def project(gathered, groups, kept_arrays):
        shapes, far = [], []
        for i, (acts, cot) in enumerate(groups):
            size = len(acts) * eval_columns + (0 if cot is None else columns) + HD
            shapes += [((tokens, size), BF), ((tokens, size), F32)]
            far += [i > 0] * 2
        shapes += [((tokens, half), BF)] * len(kept_arrays)
        far += [True] * len(kept_arrays)
        outs = pl.pallas_call(
            functools.partial(project_body, groups, kept_arrays, far, rows),
            out_shape=[
                pltpu.HBM(*shape) if is_far else jax.ShapeDtypeStruct(*shape)
                for shape, is_far in zip(shapes, far)
            ],
            in_specs=[VMEM] * 5,
            out_specs=[HBM if is_far else VMEM for is_far in far],
            scratch_shapes=[pltpu.VMEM(*shape) for shape, is_far in zip(shapes, far) if is_far]
            + [pltpu.SemaphoreType.DMA((sum(far),))],
            compiler_params=PARAMS,
        )(gathered, norm_gain, query_mat, kv_mat, output_mat)
        pairs = [(outs[2 * i], outs[2 * i + 1]) for i in range(len(groups))]
        return pairs, outs[2 * len(groups) :]

    def exchange(message):
        return lax.ppermute(message, "section", mirror)

    def attend(plan, pieces, stash, gain_before):
        last = plan["last"]
        lanes = half + (half // rows if last else 0)
        shapes = [
            jax.ShapeDtypeStruct((shards, 2 * rows, lanes), BF),
            jax.ShapeDtypeStruct((tokens, half), BF),
            jax.ShapeDtypeStruct((tokens, columns), BF),
            jax.ShapeDtypeStruct((tokens, columns), BF),
            jax.ShapeDtypeStruct((2 * HD, tokens), BF),
        ]
        if not last:
            shapes.append(jax.ShapeDtypeStruct((1, half), F32))
        extra = [gain_before] if last else []
        return pl.pallas_call(
            functools.partial(attend_body, {**plan, "outs": len(shapes)}, len(pieces)),
            out_shape=[pltpu.HBM(shape.shape, shape.dtype) for shape in shapes],
            in_specs=[VMEM] * (5 + len(pieces) + len(extra)),
            out_specs=[HBM] * len(shapes),
            scratch_shapes=[pltpu.VMEM(shape.shape, shape.dtype) for shape in shapes]
            + [pltpu.SemaphoreType.DMA((len(shapes),))],
            compiler_params=PARAMS,
        )(*pieces, stash, norm_gain, query_mat, kv_mat, output_mat, *extra)

    def reduce_blocks(block):
        received = lax.all_to_all(block, "tp", split_axis=0, concat_axis=0, tiled=True)
        return jnp.sum(received.astype(F32), axis=0)

    def reduce_kv(blocks):
        parts = blocks.reshape(2, 2, HD // 2, -1)
        low, high = parts[:, 0], parts[:, 1]
        got = lax.ppermute(jnp.where(even, high, low), "tp", swap_cores)
        chip = (jnp.where(even, low, high).astype(F32) + got.astype(F32)).astype(BF)
        sends = (
            jnp.where(second_chip, chip[1], chip[0]),
            jnp.where(second_chip, chip[0], chip[1]),
        )
        arrived = [
            lax.ppermute(send, "tp", [(b, a) for a, b in route])
            for send, route in zip(sends, kv_routes)
        ]
        return (arrived[0].astype(F32) + arrived[1].astype(F32)).astype(BF)

    last = sections // 2 - 1
    ahead = [(i, i + 1) for i in range(last)] + [
        (sections - 1 - i, sections - 2 - i) for i in range(last)
    ]
    behind = [(b, a) for a, b in ahead]
    first_layer = (section == 0) | (section == sections - 1)
    last_layer = (section == last) | (section == last + 1)

    gathered = gather_two_level(held)
    kept_arrays = tuple(range(1, 2 + ticks))
    groups = [((0, 2), 1)] + [((2 + k,), None) for k in range(1, ticks)]
    projected, (cots, *stash) = project(gathered, groups, kept_arrays)
    (message, own_x), later = projected[0], projected[1:]
    got_x = exchange(message)
    all_cots = [cots]
    act_rows, cot_rows = held[0], held[1]
    gain_total = None
    out_rows, back_rows = [], []
    all_normed, all_query_back, all_kv_back, all_mixed = [], [], [], []
    for k in range(ticks):
        first = k == 0
        plan = {
            "last": k + 1 == ticks,
            "rows": rows,
            "count_x": 2 if first else 1,
            "place_s": 1 if first else 0,
            "count_s": 2 if first else 1,
            "cot_s": first,
        }
        block, normed, query_back, mixed, kv_back, *rest = attend(
            plan,
            (own_x, got_x) if first else (own_x, got_x, own_s, got_s),
            stash[k],
            gain_total,
        )
        if k + 1 < ticks:
            gain_total = rest[0] if gain_total is None else gain_total + rest[0]
        total = reduce_blocks(block)
        layer_out = (act_rows.astype(F32) + total[:rows, :half]).astype(BF)
        back_input = (cot_rows.astype(F32) + total[rows:, :half]).astype(BF)
        out_rows.append(layer_out)
        back_rows.append(back_input)
        all_kv_back.append(kv_back)
        all_normed.append(normed)
        all_query_back.append(query_back)
        all_mixed.append(mixed)
        if k + 1 < ticks:
            f = layer_out.reshape(2, 2, row_count, half)
            b = back_input.reshape(2, 2, row_count, half)
            going_up = jnp.stack([f[0, 0], f[1, 1], b[1, 0], b[0, 1]])
            going_down = jnp.stack([f[1, 0], f[0, 1], b[0, 0], b[1, 1]])
            going_up, going_down = lax.optimization_barrier((going_up, going_down))
            from_below = lax.ppermute(going_up, "section", ahead)
            from_above = lax.ppermute(going_down, "section", behind)
            from_below, from_above = lax.optimization_barrier((from_below, from_above))
            fresh = jnp.stack(
                [fresh_acts[0, k], fresh_acts[1, k], fresh_grads[0, k], fresh_grads[1, k]]
            )
            fresh = halves(fresh)[0]
            lo = jnp.where(first_layer, fresh, from_below)
            hi = jnp.where(last_layer, going_up, from_above)
            act_rows = jnp.concatenate([lo[0], hi[1], hi[0], lo[1]], axis=0)
            cot_rows = jnp.concatenate([hi[2], lo[3], lo[2], hi[3]], axis=0)
            entering = jnp.stack([act_rows, cot_rows])
            entering, message_s = lax.optimization_barrier((entering, later[k][0]))
            own_s, got_s = later[k][1], exchange(message_s)
            act_rows, cot_rows = entering[0], entering[1]
            moved = gather(entering)
            moved, got_s = lax.optimization_barrier((moved, got_s))
            ((message, own_x),), (cots,) = project(moved, [((0,), 1)], (1,))
            all_cots.append(cots)
            got_x = exchange(message)

    normed = jnp.concatenate(all_normed, axis=0)
    grad_query = t_mm(normed, jnp.concatenate(all_query_back, axis=0)).astype(BF)
    grad_keyval = mm(reduce_kv(jnp.concatenate(all_kv_back, axis=1)), normed).astype(BF).T
    grad_output = t_mm(
        jnp.concatenate(all_cots, axis=0), jnp.concatenate(all_mixed, axis=0)
    ).astype(BF)
    gain_lanes = total[:, half:]
    grad_gain = (gain_lanes[:rows] + gain_lanes[rows:]).astype(BF).reshape(half)

    leaving = jnp.stack(out_rows + back_rows).reshape(2 * ticks, 2, 2 * row_count, half)
    lo_rows, hi_rows = leaving[:, 0], leaving[:, 1]
    mine, theirs = jnp.where(lower, lo_rows, hi_rows), jnp.where(lower, hi_rows, lo_rows)
    returned = lax.ppermute(theirs, "section", mirror)
    whole = jnp.concatenate(
        [jnp.where(lower, mine, returned), jnp.where(lower, returned, mine)], axis=2
    ).reshape(2, ticks, 2, row_count, width)
    whole = whole.transpose(0, 2, 1, 3, 4)
    return (
        whole[0][None],
        whole[1][None],
        grad_query[None],
        grad_keyval[None],
        grad_output[None],
        grad_gain[None],
    )


def solution(mesh):
    in_specs = (
        P("section", None, "tp", None),
        P(None, None, "tp", None),
        P("section", None, None, "tp", None),
        P("section", None, "tp", None),
        P(None, None, "tp", None),
        P("section", None),
        P("section", None, "tp"),
        P("section", None, "tp"),
        P("section", "tp", None),
    )
    out_specs = (
        P("section", None, None, "tp", None),
        P("section", None, None, "tp", None),
        P("section", None, "tp"),
        P("section", None, "tp"),
        P("section", None, "tp"),
        P("section", None),
    )
    return jax.shard_map(
        on_device, mesh=mesh, in_specs=in_specs, out_specs=out_specs, check_vma=False
    )
```

```python
import functools
import math

import jax
import jax.numpy as jnp
from jax import lax
from jax.experimental import pallas as pl
from jax.experimental.pallas import tpu as pltpu
from jax.sharding import PartitionSpec as P

HD = 128
KVH = 4
EPSILON = 1e-05
BF = jnp.bfloat16
F32 = jnp.float32


def mm(left, right, dims=((1,), (0,))):
    return lax.dot_general(left, right, (dims, ((), ())), preferred_element_type=F32)


def mm_t(left, right):
    return mm(left, right, ((1,), (1,)))


def t_mm(left, right):
    return mm(left, right, ((0,), (0,)))


def pair_mask(tokens, row_count):
    def parts(axis):
        i = lax.broadcasted_iota(jnp.int32, (tokens, tokens), axis)
        group = (i // row_count) % 4
        return group, (i // (4 * row_count)) * row_count + i % row_count

    (query_group, query_time), (key_group, key_time) = parts(0), parts(1)
    return (query_group == key_group) & (key_time <= query_time)


def array_of(gathered_ref, index, rows):
    part = gathered_ref[...].astype(F32)[:, index * rows : (index + 1) * rows]
    return part.reshape(part.shape[0] * rows, part.shape[2])


def lane_sum(block, lanes):
    lane = lax.broadcasted_iota(jnp.int32, block.shape, 1)
    chosen = functools.reduce(jnp.logical_or, [lane == i for i in lanes])
    return jnp.sum(jnp.where(chosen, block, 0.0), axis=1, keepdims=True)


def project_body(groups, kept_arrays, far, rows, gathered, gain, query_mat, kv_mat, output_mat, *rest):
    results, buffers, sems = rest[: len(far)], rest[len(far) : -1], rest[-1]
    places = [i for i, is_far in enumerate(far) if is_far]
    outs = [buffers[places.index(i)] if is_far else results[i] for i, is_far in enumerate(far)]
    copies = []

    def send(index):
        if far[index]:
            place = places.index(index)
            copies.append(pltpu.make_async_copy(buffers[place], results[index], sems.at[place]))
            copies[-1].start()

    for i, kept_array in enumerate(kept_arrays):
        index = 2 * len(groups) + i
        outs[index][...] = array_of(gathered, kept_array, rows).astype(BF)
        send(index)
    gain_row = gain[...].astype(F32)
    for index, (acts, cot) in enumerate(groups):
        message, own = outs[2 * index], outs[2 * index + 1]
        tokens = own.shape[0]
        at = 0
        squares = []
        for act in acts:
            wide = array_of(gathered, act, rows)
            scaled = (wide * gain_row).astype(BF)
            squares.append(jnp.sum(wide * wide, axis=1, keepdims=True))
            for part in (mm(scaled, query_mat[...]), mm_t(scaled, kv_mat[...])):
                own[:, at : at + part.shape[1]] = part
                message[:, at : at + part.shape[1]] = part.astype(BF)
                at += part.shape[1]
        if cot is not None:
            part = mm_t(array_of(gathered, cot, rows).astype(BF), output_mat[...])
            own[:, at : at + part.shape[1]] = part
            message[:, at : at + part.shape[1]] = part.astype(BF)
            at += part.shape[1]
        lane = lax.broadcasted_iota(jnp.int32, (tokens, HD), 1)
        kept = jnp.zeros((tokens, HD), F32)
        sent = jnp.zeros((tokens, HD), F32)
        for i, square in enumerate(squares):
            high = square.astype(BF).astype(F32)
            kept = jnp.where(lane == i, square, kept)
            sent = jnp.where(lane == i, high, sent)
            sent = jnp.where(lane == len(squares) + i, square - high, sent)
        own[:, at : at + HD] = kept
        message[:, at : at + HD] = sent.astype(BF)
        send(2 * index)
        send(2 * index + 1)
    for copy in copies:
        copy.wait()


def stack_heads(columns):
    return jnp.concatenate([columns[:, i : i + HD] for i in range(0, columns.shape[1], HD)], axis=0)


def unstack_heads(stacked, tokens):
    return jnp.concatenate(
        [stacked[i : i + tokens] for i in range(0, stacked.shape[0], tokens)], axis=1
    )


def softmax_of(stacked, keys, mask):
    scores = mm_t(stacked, keys) / math.sqrt(HD)
    scores = jnp.where(mask, scores, -jnp.inf)
    weights = jnp.exp(scores - jnp.max(scores, axis=1, keepdims=True))
    return weights / jnp.sum(weights, axis=1, keepdims=True)


def attend_body(
    plan, pieces, core, own_x, got_x, *rest
):
    last = plan["last"]
    own_s, got_s = (own_x, got_x) if pieces == 2 else rest[: pieces - 2]
    stash, gain, query_mat, kv_mat, output_mat, *rest = rest[pieces - 2 :]
    if last:
        gain_before, rest = rest[0], rest[1:]
    outs, sems = rest[: plan["outs"]], rest[-1]
    block, other_block = rest[plan["outs"]], rest[plan["outs"] + 1]
    leaving = []

    def leave(index, value):
        buffer = rest[plan["outs"] + index]
        buffer[...] = value
        send(index)

    def send(index):
        copy = pltpu.make_async_copy(
            rest[plan["outs"] + index], outs[index], sems.at[index]
        )
        copy.start()
        leaving.append(copy)
    rows, columns = plan["rows"], query_mat.shape[1]
    shards = 2 * block.shape[0]
    tokens, half = shards * rows, query_mat.shape[0]
    eval_columns = columns + 2 * HD
    heads = columns // HD

    def total(own, got, at, size):
        return own[:, at : at + size] + got[:, at : at + size].astype(F32)

    def projected(own, got, place, count, has_cot):
        at = count * eval_columns + (columns if has_cot else 0)
        square = lane_sum(total(own, got, at, HD), (place, count + place))
        inverse = lax.rsqrt(square / (2 * half) + EPSILON)
        start = place * eval_columns
        queries = total(own, got, start, columns) * inverse
        keyvals = total(own, got, start + columns, 2 * HD) * inverse
        return queries, keyvals, inverse

    mask = pair_mask(tokens, rows // 4)
    mask = jnp.concatenate([mask.astype(jnp.int32)] * heads, axis=0) == 1

    queries, keyvals, _ = projected(own_x, got_x, 0, plan["count_x"], True)
    keys, values = keyvals[:, :HD].astype(BF), keyvals[:, HD:].astype(BF)
    probs = softmax_of(stack_heads(queries).astype(BF), keys, mask)
    mixed = unstack_heads(mm(probs.astype(BF), values), tokens).astype(BF)
    out_part = mm(mixed, output_mat[...])

    back_mixed = total(own_x, got_x, plan["count_x"] * eval_columns, columns)
    queries, keyvals, inverse = projected(
        own_s, got_s, plan["place_s"], plan["count_s"], plan["cot_s"]
    )
    keys, values = keyvals[:, :HD].astype(BF), keyvals[:, HD:].astype(BF)
    stacked = stack_heads(queries).astype(BF)
    probs = softmax_of(stacked, keys, mask)
    leave(4, unstack_heads(mm(probs.astype(BF), values), tokens).astype(BF))
    back = stack_heads(back_mixed).astype(BF)
    back_probs = mm_t(back, values)
    inner = jnp.sum(probs * back_probs, axis=1, keepdims=True)
    back_scores = probs * (back_probs - inner) / math.sqrt(HD)
    query_back = unstack_heads(mm(back_scores.astype(BF), keys), tokens).astype(BF)
    leave(3, query_back)
    key_back = mm(back_scores.T.astype(BF), stacked)
    value_back = mm(probs.T.astype(BF), back)
    keyval_back = jnp.concatenate([key_back, value_back], axis=1).astype(BF)
    leave(5, jnp.concatenate([key_back.T, value_back.T], axis=0).astype(BF))

    back_normed = mm_t(query_back, query_mat[...]) + mm(keyval_back, kv_mat[...])
    along = jnp.sum(query_back.astype(F32) * queries, axis=1, keepdims=True) + jnp.sum(
        keyval_back.astype(F32) * keyvals, axis=1, keepdims=True
    )
    gain_row = gain[...].astype(F32)
    unit = stash[...].astype(F32) * inverse
    leave(2, (unit * gain_row).astype(BF))
    back_part = inverse * (back_normed * gain_row - unit * (along / (2 * half)))
    gain_part = jnp.sum(back_normed * unit, axis=0, keepdims=True)

    both = jnp.concatenate(
        [out_part.reshape(shards, rows, half), back_part.reshape(shards, rows, half)], axis=1
    )
    both = both.reshape(shards // 2, 2, 2 * rows, half)
    for target, parity in ((block, 0), (other_block, 1)):
        part = jnp.where(core[0] == parity, both[:, 0], both[:, 1])
        target[:, :, :half] = part.astype(BF)

    if last:
        gain_part = gain_part + gain_before[...]
        high = gain_part.astype(BF).astype(F32)
        width = half // rows
        spread = jnp.concatenate(
            [part[:, i * width : (i + 1) * width] for part in (high, gain_part - high) for i in range(rows)],
            axis=0,
        ).astype(BF)
        for d in range(shards // 2):
            block[d, :, half:] = spread
            other_block[d, :, half:] = spread
    else:
        leave(6, gain_part)
    send(0)
    send(1)
    for copy in leaving:
        copy.wait()


VMEM = pl.BlockSpec(memory_space=pltpu.VMEM)
SMEM = pl.BlockSpec(memory_space=pltpu.SMEM)
HBM = pl.BlockSpec(memory_space=pltpu.HBM)
PARAMS = pltpu.CompilerParams(vmem_limit_bytes=24 * 2**20)


def on_device(
    carried_acts,
    fresh_acts,
    stashed_acts,
    carried_grads,
    fresh_grads,
    norm_gain,
    query_weight,
    keyval_weight,
    output_weight,
):
    sections = lax.axis_size("section")
    shards = lax.axis_size("tp")
    section = lax.axis_index("section")
    me = lax.axis_index("tp")
    lower = section < sections // 2
    ticks = stashed_acts.shape[2]
    width = carried_acts.shape[3]
    half = width // 2
    row_count = carried_acts.shape[2]
    rows = 4 * row_count
    tokens = rows * shards
    query_mat, output_mat = query_weight[0], output_weight[0]
    columns = query_mat.shape[1]
    mirror = [(i, sections - 1 - i) for i in range(sections)]
    kv_group = shards // KVH

    def halves(whole):
        first, second = whole[..., :half], whole[..., half:]
        return jnp.where(lower, first, second), jnp.where(lower, second, first)

    entering = jnp.stack(
        [carried_acts[0], carried_grads[0]] + [stashed_acts[0, :, k] for k in range(ticks)]
    ).reshape(ticks + 2, 2 * row_count, width)
    own, other = halves(entering)
    arrived = lax.ppermute(other, "section", mirror)
    held = jnp.concatenate(
        [jnp.where(lower, own, arrived), jnp.where(lower, arrived, own)], axis=1
    )

    kv_own = keyval_weight[0].T
    sources = [[2 * j, 2 * j + 1, shards // 2 + 2 * j, shards // 2 + 2 * j + 1] for j in range(KVH)]
    kv_routes = [
        [
            (sources[j][(i + 2 * k) % kv_group], kv_group * j + i)
            for j in range(KVH)
            for i in range(kv_group)
        ]
        for k in range(2)
    ]
    swap_cores = [(i, i ^ 1) for i in range(shards)]
    fetched = [lax.ppermute(kv_own, "tp", route) for route in kv_routes]
    held, fetched = lax.optimization_barrier((held, fetched))
    second_chip = (me // 2) % 2 == 1
    mine = jnp.stack(
        [
            jnp.where(second_chip, fetched[1], fetched[0]),
            jnp.where(second_chip, fetched[0], fetched[1]),
        ]
    )
    swapped = lax.ppermute(mine, "tp", swap_cores)
    even = me % 2 == 0
    kv_mat = jnp.stack(
        [jnp.where(even, mine, swapped), jnp.where(even, swapped, mine)], axis=1
    ).reshape(2 * HD, half)

    same_core = [[2 * chip + core for chip in range(shards // 2)] for core in range(2)]

    def gather(local):
        count, chips = local.shape[0], shards // 2
        spread = jnp.broadcast_to(local.reshape(1, count * rows, half), (chips, count * rows, half))
        mine = lax.all_to_all(
            spread, "tp", split_axis=0, concat_axis=0, axis_index_groups=same_core, tiled=True
        )
        other = lax.ppermute(mine, "tp", swap_cores)
        both = jnp.stack(
            [jnp.where(even, mine, other), jnp.where(even, other, mine)], axis=1
        )
        return both.reshape(shards, count * rows, half)

    eval_columns = columns + 2 * HD

    def project(gathered, groups, kept_arrays):
        shapes, far = [], []
        for i, (acts, cot) in enumerate(groups):
            size = len(acts) * eval_columns + (0 if cot is None else columns) + HD
            shapes += [((tokens, size), BF), ((tokens, size), F32)]
            far += [i > 0] * 2
        shapes += [((tokens, half), BF)] * len(kept_arrays)
        far += [True] * len(kept_arrays)
        outs = pl.pallas_call(
            functools.partial(project_body, groups, kept_arrays, far, rows),
            out_shape=[
                pltpu.HBM(*shape) if is_far else jax.ShapeDtypeStruct(*shape)
                for shape, is_far in zip(shapes, far)
            ],
            in_specs=[VMEM] * 5,
            out_specs=[HBM if is_far else VMEM for is_far in far],
            scratch_shapes=[pltpu.VMEM(*shape) for shape, is_far in zip(shapes, far) if is_far]
            + [pltpu.SemaphoreType.DMA((sum(far),))],
            compiler_params=PARAMS,
        )(gathered, norm_gain, query_mat, kv_mat, output_mat)
        pairs = [(outs[2 * i], outs[2 * i + 1]) for i in range(len(groups))]
        return pairs, outs[2 * len(groups) :]

    def exchange(message):
        return lax.ppermute(message, "section", mirror)

    def attend(plan, pieces, stash, gain_before):
        last = plan["last"]
        lanes = half + (half // rows if last else 0)
        shapes = [
            jax.ShapeDtypeStruct((shards // 2, 2 * rows, lanes), BF),
            jax.ShapeDtypeStruct((shards // 2, 2 * rows, lanes), BF),
            jax.ShapeDtypeStruct((tokens, half), BF),
            jax.ShapeDtypeStruct((tokens, columns), BF),
            jax.ShapeDtypeStruct((tokens, columns), BF),
            jax.ShapeDtypeStruct((2 * HD, tokens), BF),
        ]
        if not last:
            shapes.append(jax.ShapeDtypeStruct((1, half), F32))
        extra = [gain_before] if last else []
        return pl.pallas_call(
            functools.partial(attend_body, {**plan, "outs": len(shapes)}, len(pieces)),
            out_shape=[pltpu.HBM(shape.shape, shape.dtype) for shape in shapes],
            in_specs=[SMEM] + [VMEM] * (5 + len(pieces) + len(extra)),
            out_specs=[HBM] * len(shapes),
            scratch_shapes=[pltpu.VMEM(shape.shape, shape.dtype) for shape in shapes]
            + [pltpu.SemaphoreType.DMA((len(shapes),))],
            compiler_params=PARAMS,
        )(core, *pieces, stash, norm_gain, query_mat, kv_mat, output_mat, *extra)

    core = (me % 2).astype(jnp.int32).reshape(1)

    def reduce_blocks(mine, other, beside=None):
        got = lax.ppermute(other, "tp", swap_cores)
        chip = (mine.astype(F32) + got.astype(F32)).astype(BF)
        if beside is not None:
            chip, beside = lax.optimization_barrier((chip, beside))
            beside = exchange(beside)
        received = lax.all_to_all(
            chip, "tp", split_axis=0, concat_axis=0, axis_index_groups=same_core, tiled=True
        )
        if beside is not None:
            received, beside = lax.optimization_barrier((received, beside))
        return jnp.sum(received.astype(F32), axis=0), beside

    def reduce_kv(blocks):
        parts = blocks.reshape(2, 2, HD // 2, -1)
        low, high = parts[:, 0], parts[:, 1]
        got = lax.ppermute(jnp.where(even, high, low), "tp", swap_cores)
        chip = (jnp.where(even, low, high).astype(F32) + got.astype(F32)).astype(BF)
        sends = (
            jnp.where(second_chip, chip[1], chip[0]),
            jnp.where(second_chip, chip[0], chip[1]),
        )
        arrived = [
            lax.ppermute(send, "tp", [(b, a) for a, b in route])
            for send, route in zip(sends, kv_routes)
        ]
        return (arrived[0].astype(F32) + arrived[1].astype(F32)).astype(BF)

    last = sections // 2 - 1
    ahead = [(i, i + 1) for i in range(last)] + [
        (sections - 1 - i, sections - 2 - i) for i in range(last)
    ]
    behind = [(b, a) for a, b in ahead]
    first_layer = (section == 0) | (section == sections - 1)
    last_layer = (section == last) | (section == last + 1)

    gathered = gather(held)
    kept_arrays = tuple(range(1, 2 + ticks))
    groups = [((0, 2), 1)] + [((2 + k,), None) for k in range(1, ticks)]
    projected, (cots, *stash) = project(gathered, groups, kept_arrays)
    (message, own_x), later = projected[0], projected[1:]
    got_x = exchange(message)
    all_cots = [cots]
    act_rows, cot_rows = held[0], held[1]
    gain_total = None
    out_rows, back_rows = [], []
    all_normed, all_query_back, all_kv_back, all_mixed = [], [], [], []
    for k in range(ticks):
        first = k == 0
        plan = {
            "last": k + 1 == ticks,
            "rows": rows,
            "count_x": 2 if first else 1,
            "place_s": 1 if first else 0,
            "count_s": 2 if first else 1,
            "cot_s": first,
        }
        mine, other, normed, query_back, mixed, kv_back, *rest = attend(
            plan,
            (own_x, got_x) if first else (own_x, got_x, own_s, got_s),
            stash[k],
            gain_total,
        )
        if k + 1 < ticks:
            gain_total = rest[0] if gain_total is None else gain_total + rest[0]
        message_s = None if k + 1 == ticks else later[k][0]
        total, arrived_s = reduce_blocks(mine, other, message_s)
        layer_out = (act_rows.astype(F32) + total[:rows, :half]).astype(BF)
        back_input = (cot_rows.astype(F32) + total[rows:, :half]).astype(BF)
        out_rows.append(layer_out)
        back_rows.append(back_input)
        all_kv_back.append(kv_back)
        all_normed.append(normed)
        all_query_back.append(query_back)
        all_mixed.append(mixed)
        if k + 1 < ticks:
            f = layer_out.reshape(2, 2, row_count, half)
            b = back_input.reshape(2, 2, row_count, half)
            going_up = jnp.stack([f[0, 0], f[1, 1], b[1, 0], b[0, 1]])
            going_down = jnp.stack([f[1, 0], f[0, 1], b[0, 0], b[1, 1]])
            going_up, going_down = lax.optimization_barrier((going_up, going_down))
            from_below = lax.ppermute(going_up, "section", ahead)
            from_above = lax.ppermute(going_down, "section", behind)
            from_below, from_above = lax.optimization_barrier((from_below, from_above))
            fresh = jnp.stack(
                [fresh_acts[0, k], fresh_acts[1, k], fresh_grads[0, k], fresh_grads[1, k]]
            )
            fresh = halves(fresh)[0]
            lo = jnp.where(first_layer, fresh, from_below)
            hi = jnp.where(last_layer, going_up, from_above)
            act_rows = jnp.concatenate([lo[0], hi[1], hi[0], lo[1]], axis=0)
            cot_rows = jnp.concatenate([hi[2], lo[3], lo[2], hi[3]], axis=0)
            entering = jnp.stack([act_rows, cot_rows])
            own_s, got_s = later[k][1], arrived_s
            act_rows, cot_rows = entering[0], entering[1]
            moved = gather(entering)
            ((message, own_x),), (cots,) = project(moved, [((0,), 1)], (1,))
            all_cots.append(cots)
            got_x = exchange(message)

    normed = jnp.concatenate(all_normed, axis=0)
    total, *late = lax.optimization_barrier((total, *all_query_back, *all_mixed))
    all_query_back, all_mixed = late[:ticks], late[ticks:]
    grad_query = t_mm(normed, jnp.concatenate(all_query_back, axis=0)).astype(BF)
    grad_keyval = mm(reduce_kv(jnp.concatenate(all_kv_back, axis=1)), normed).astype(BF).T
    grad_output = t_mm(
        jnp.concatenate(all_cots, axis=0), jnp.concatenate(all_mixed, axis=0)
    ).astype(BF)
    gain_lanes = total[:, half:]
    grad_gain = (gain_lanes[:rows] + gain_lanes[rows:]).astype(BF).reshape(half)

    leaving = jnp.stack(out_rows + back_rows).reshape(2 * ticks, 2, 2 * row_count, half)
    lo_rows, hi_rows = leaving[:, 0], leaving[:, 1]
    mine, theirs = jnp.where(lower, lo_rows, hi_rows), jnp.where(lower, hi_rows, lo_rows)
    returned = lax.ppermute(theirs, "section", mirror)
    whole = jnp.concatenate(
        [jnp.where(lower, mine, returned), jnp.where(lower, returned, mine)], axis=2
    ).reshape(2, ticks, 2, row_count, width)
    whole = whole.transpose(0, 2, 1, 3, 4)
    return (
        whole[0][None],
        whole[1][None],
        grad_query[None],
        grad_keyval[None],
        grad_output[None],
        grad_gain[None],
    )


def solution(mesh):
    in_specs = (
        P("section", None, "tp", None),
        P(None, None, "tp", None),
        P("section", None, None, "tp", None),
        P("section", None, "tp", None),
        P(None, None, "tp", None),
        P("section", None),
        P("section", None, "tp"),
        P("section", None, "tp"),
        P("section", "tp", None),
    )
    out_specs = (
        P("section", None, None, "tp", None),
        P("section", None, None, "tp", None),
        P("section", None, "tp"),
        P("section", None, "tp"),
        P("section", None, "tp"),
        P("section", None),
    )
    return jax.shard_map(
        on_device, mesh=mesh, in_specs=in_specs, out_specs=out_specs, check_vma=False
    )
```

```python
import functools
import math

import jax
import jax.numpy as jnp
from jax import lax
from jax.experimental import pallas as pl
from jax.experimental.pallas import tpu as pltpu
from jax.sharding import PartitionSpec as P

HD = 128
KVH = 4
EPSILON = 1e-05
BF = jnp.bfloat16
F32 = jnp.float32


def mm(left, right, dims=((1,), (0,))):
    return lax.dot_general(left, right, (dims, ((), ())), preferred_element_type=F32)


def mm_t(left, right):
    return mm(left, right, ((1,), (1,)))


def t_mm(left, right):
    return mm(left, right, ((0,), (0,)))


def pair_mask(tokens, row_count):
    def parts(axis):
        i = lax.broadcasted_iota(jnp.int32, (tokens, tokens), axis)
        group = (i // row_count) % 4
        return group, (i // (4 * row_count)) * row_count + i % row_count

    (query_group, query_time), (key_group, key_time) = parts(0), parts(1)
    return (query_group == key_group) & (key_time <= query_time)


def array_of(gathered_ref, index, rows):
    part = gathered_ref[...].astype(F32)[:, index * rows : (index + 1) * rows]
    return part.reshape(part.shape[0] * rows, part.shape[2])


def lane_sum(block, lanes):
    lane = lax.broadcasted_iota(jnp.int32, block.shape, 1)
    chosen = functools.reduce(jnp.logical_or, [lane == i for i in lanes])
    return jnp.sum(jnp.where(chosen, block, 0.0), axis=1, keepdims=True)


def project_body(groups, kept_arrays, far, rows, gathered, gain, query_mat, kv_mat, output_mat, *rest):
    results, buffers, sems = rest[: len(far)], rest[len(far) : -1], rest[-1]
    places = [i for i, is_far in enumerate(far) if is_far]
    outs = [buffers[places.index(i)] if is_far else results[i] for i, is_far in enumerate(far)]
    copies = []

    def send(index):
        if far[index]:
            place = places.index(index)
            copies.append(pltpu.make_async_copy(buffers[place], results[index], sems.at[place]))
            copies[-1].start()

    for i, kept_array in enumerate(kept_arrays):
        index = 2 * len(groups) + i
        outs[index][...] = array_of(gathered, kept_array, rows).astype(BF)
        send(index)
    gain_row = gain[...].astype(F32)
    for index, (acts, cot) in enumerate(groups):
        message, own = outs[2 * index], outs[2 * index + 1]
        tokens = own.shape[0]
        at = 0
        squares = []
        for act in acts:
            wide = array_of(gathered, act, rows)
            scaled = (wide * gain_row).astype(BF)
            squares.append(jnp.sum(wide * wide, axis=1, keepdims=True))
            for part in (mm(scaled, query_mat[...]), mm_t(scaled, kv_mat[...])):
                own[:, at : at + part.shape[1]] = part
                message[:, at : at + part.shape[1]] = part.astype(BF)
                at += part.shape[1]
        if cot is not None:
            part = mm_t(array_of(gathered, cot, rows).astype(BF), output_mat[...])
            own[:, at : at + part.shape[1]] = part
            message[:, at : at + part.shape[1]] = part.astype(BF)
            at += part.shape[1]
        lane = lax.broadcasted_iota(jnp.int32, (tokens, HD), 1)
        kept = jnp.zeros((tokens, HD), F32)
        sent = jnp.zeros((tokens, HD), F32)
        for i, square in enumerate(squares):
            high = square.astype(BF).astype(F32)
            kept = jnp.where(lane == i, square, kept)
            sent = jnp.where(lane == i, high, sent)
            sent = jnp.where(lane == len(squares) + i, square - high, sent)
        own[:, at : at + HD] = kept
        message[:, at : at + HD] = sent.astype(BF)
        send(2 * index)
        send(2 * index + 1)
    for copy in copies:
        copy.wait()


def stack_heads(columns):
    return jnp.concatenate([columns[:, i : i + HD] for i in range(0, columns.shape[1], HD)], axis=0)


def unstack_heads(stacked, tokens):
    return jnp.concatenate(
        [stacked[i : i + tokens] for i in range(0, stacked.shape[0], tokens)], axis=1
    )


def softmax_of(stacked, keys, mask):
    scores = mm_t(stacked, keys) / math.sqrt(HD)
    scores = jnp.where(mask, scores, -jnp.inf)
    weights = jnp.exp(scores - jnp.max(scores, axis=1, keepdims=True))
    return weights / jnp.sum(weights, axis=1, keepdims=True)


def attend_body(
    plan, pieces, core, own_x, got_x, *rest
):
    last = plan["last"]
    own_s, got_s = (own_x, got_x) if pieces == 2 else rest[: pieces - 2]
    stash, gain, query_mat, kv_mat, output_mat, *rest = rest[pieces - 2 :]
    if last:
        gain_before, rest = rest[0], rest[1:]
    outs, sems = rest[: plan["outs"]], rest[-1]
    block, other_block = outs[:2]
    leaving = []

    def leave(index, value):
        buffer = rest[plan["outs"] + index - 2]
        buffer[...] = value
        copy = pltpu.make_async_copy(buffer, outs[index], sems.at[index - 2])
        copy.start()
        leaving.append(copy)
    rows, columns = plan["rows"], query_mat.shape[1]
    shards = 2 * block.shape[0]
    tokens, half = shards * rows, query_mat.shape[0]
    eval_columns = columns + 2 * HD
    heads = columns // HD

    def total(own, got, at, size):
        return own[:, at : at + size] + got[:, at : at + size].astype(F32)

    def projected(own, got, place, count, has_cot):
        at = count * eval_columns + (columns if has_cot else 0)
        square = lane_sum(total(own, got, at, HD), (place, count + place))
        inverse = lax.rsqrt(square / (2 * half) + EPSILON)
        start = place * eval_columns
        queries = total(own, got, start, columns) * inverse
        keyvals = total(own, got, start + columns, 2 * HD) * inverse
        return queries, keyvals, inverse

    mask = pair_mask(tokens, rows // 4)
    mask = jnp.concatenate([mask.astype(jnp.int32)] * heads, axis=0) == 1

    queries, keyvals, _ = projected(own_x, got_x, 0, plan["count_x"], True)
    keys, values = keyvals[:, :HD].astype(BF), keyvals[:, HD:].astype(BF)
    probs = softmax_of(stack_heads(queries).astype(BF), keys, mask)
    mixed = unstack_heads(mm(probs.astype(BF), values), tokens).astype(BF)
    out_part = mm(mixed, output_mat[...])

    back_mixed = total(own_x, got_x, plan["count_x"] * eval_columns, columns)
    queries, keyvals, inverse = projected(
        own_s, got_s, plan["place_s"], plan["count_s"], plan["cot_s"]
    )
    keys, values = keyvals[:, :HD].astype(BF), keyvals[:, HD:].astype(BF)
    stacked = stack_heads(queries).astype(BF)
    probs = softmax_of(stacked, keys, mask)
    leave(4, unstack_heads(mm(probs.astype(BF), values), tokens).astype(BF))
    back = stack_heads(back_mixed).astype(BF)
    back_probs = mm_t(back, values)
    inner = jnp.sum(probs * back_probs, axis=1, keepdims=True)
    back_scores = probs * (back_probs - inner) / math.sqrt(HD)
    query_back = unstack_heads(mm(back_scores.astype(BF), keys), tokens).astype(BF)
    leave(3, query_back)
    key_back = mm(back_scores.T.astype(BF), stacked)
    value_back = mm(probs.T.astype(BF), back)
    keyval_back = jnp.concatenate([key_back, value_back], axis=1).astype(BF)
    leave(5, jnp.concatenate([key_back.T, value_back.T], axis=0).astype(BF))

    back_normed = mm_t(query_back, query_mat[...]) + mm(keyval_back, kv_mat[...])
    along = jnp.sum(query_back.astype(F32) * queries, axis=1, keepdims=True) + jnp.sum(
        keyval_back.astype(F32) * keyvals, axis=1, keepdims=True
    )
    gain_row = gain[...].astype(F32)
    unit = stash[...].astype(F32) * inverse
    leave(2, (unit * gain_row).astype(BF))
    back_part = inverse * (back_normed * gain_row - unit * (along / (2 * half)))
    gain_part = jnp.sum(back_normed * unit, axis=0, keepdims=True)

    both = jnp.concatenate(
        [out_part.reshape(shards, rows, half), back_part.reshape(shards, rows, half)], axis=1
    )
    both = both.reshape(shards // 2, 2, 2 * rows, half)
    for target, parity in ((block, 0), (other_block, 1)):
        part = jnp.where(core[0] == parity, both[:, 0], both[:, 1])
        target[:, :, :half] = part.astype(BF)

    if last:
        gain_part = gain_part + gain_before[...]
        high = gain_part.astype(BF).astype(F32)
        width = half // rows
        spread = jnp.concatenate(
            [part[:, i * width : (i + 1) * width] for part in (high, gain_part - high) for i in range(rows)],
            axis=0,
        ).astype(BF)
        for d in range(shards // 2):
            block[d, :, half:] = spread
            other_block[d, :, half:] = spread
    else:
        leave(6, gain_part)
    for copy in leaving:
        copy.wait()


VMEM = pl.BlockSpec(memory_space=pltpu.VMEM)
SMEM = pl.BlockSpec(memory_space=pltpu.SMEM)
HBM = pl.BlockSpec(memory_space=pltpu.HBM)
PARAMS = pltpu.CompilerParams(vmem_limit_bytes=24 * 2**20)


def on_device(
    carried_acts,
    fresh_acts,
    stashed_acts,
    carried_grads,
    fresh_grads,
    norm_gain,
    query_weight,
    keyval_weight,
    output_weight,
):
    sections = lax.axis_size("section")
    shards = lax.axis_size("tp")
    section = lax.axis_index("section")
    me = lax.axis_index("tp")
    lower = section < sections // 2
    ticks = stashed_acts.shape[2]
    width = carried_acts.shape[3]
    half = width // 2
    row_count = carried_acts.shape[2]
    rows = 4 * row_count
    tokens = rows * shards
    query_mat, output_mat = query_weight[0], output_weight[0]
    columns = query_mat.shape[1]
    mirror = [(i, sections - 1 - i) for i in range(sections)]
    kv_group = shards // KVH

    def halves(whole):
        first, second = whole[..., :half], whole[..., half:]
        return jnp.where(lower, first, second), jnp.where(lower, second, first)

    entering = jnp.stack(
        [carried_acts[0], carried_grads[0]] + [stashed_acts[0, :, k] for k in range(ticks)]
    ).reshape(ticks + 2, 2 * row_count, width)
    own, other = halves(entering)
    arrived = lax.ppermute(other, "section", mirror)
    held = jnp.concatenate(
        [jnp.where(lower, own, arrived), jnp.where(lower, arrived, own)], axis=1
    )

    kv_own = keyval_weight[0].T
    sources = [[2 * j, 2 * j + 1, shards // 2 + 2 * j, shards // 2 + 2 * j + 1] for j in range(KVH)]
    kv_routes = [
        [
            (sources[j][(i + 2 * k) % kv_group], kv_group * j + i)
            for j in range(KVH)
            for i in range(kv_group)
        ]
        for k in range(2)
    ]
    swap_cores = [(i, i ^ 1) for i in range(shards)]
    fetched = [lax.ppermute(kv_own, "tp", route) for route in kv_routes]
    held, fetched = lax.optimization_barrier((held, fetched))
    second_chip = (me // 2) % 2 == 1
    mine = jnp.stack(
        [
            jnp.where(second_chip, fetched[1], fetched[0]),
            jnp.where(second_chip, fetched[0], fetched[1]),
        ]
    )
    swapped = lax.ppermute(mine, "tp", swap_cores)
    even = me % 2 == 0
    kv_mat = jnp.stack(
        [jnp.where(even, mine, swapped), jnp.where(even, swapped, mine)], axis=1
    ).reshape(2 * HD, half)

    same_core = [[2 * chip + core for chip in range(shards // 2)] for core in range(2)]

    def gather(local):
        count, chips = local.shape[0], shards // 2
        spread = jnp.broadcast_to(local.reshape(1, count * rows, half), (chips, count * rows, half))
        mine = lax.all_to_all(
            spread, "tp", split_axis=0, concat_axis=0, axis_index_groups=same_core, tiled=True
        )
        other = lax.ppermute(mine, "tp", swap_cores)
        both = jnp.stack(
            [jnp.where(even, mine, other), jnp.where(even, other, mine)], axis=1
        )
        return both.reshape(shards, count * rows, half)

    eval_columns = columns + 2 * HD

    def project(gathered, groups, kept_arrays, near=()):
        shapes, far = [], []
        for i, (acts, cot) in enumerate(groups):
            size = len(acts) * eval_columns + (0 if cot is None else columns) + HD
            shapes += [((tokens, size), BF), ((tokens, size), F32)]
            far += [i > 0] * 2
        shapes += [((tokens, half), BF)] * len(kept_arrays)
        far += [kept_array not in near for kept_array in kept_arrays]
        outs = pl.pallas_call(
            functools.partial(project_body, groups, kept_arrays, far, rows),
            out_shape=[
                pltpu.HBM(*shape) if is_far else jax.ShapeDtypeStruct(*shape)
                for shape, is_far in zip(shapes, far)
            ],
            in_specs=[VMEM] * 5,
            out_specs=[HBM if is_far else VMEM for is_far in far],
            scratch_shapes=[pltpu.VMEM(*shape) for shape, is_far in zip(shapes, far) if is_far]
            + [pltpu.SemaphoreType.DMA((sum(far),))],
            compiler_params=PARAMS,
        )(gathered, norm_gain, query_mat, kv_mat, output_mat)
        pairs = [(outs[2 * i], outs[2 * i + 1]) for i in range(len(groups))]
        return pairs, outs[2 * len(groups) :]

    def exchange(message):
        return lax.ppermute(message, "section", mirror)

    def attend(plan, pieces, stash, gain_before):
        last = plan["last"]
        lanes = half + (half // rows if last else 0)
        shapes = [
            jax.ShapeDtypeStruct((shards // 2, 2 * rows, lanes), BF),
            jax.ShapeDtypeStruct((shards // 2, 2 * rows, lanes), BF),
            jax.ShapeDtypeStruct((tokens, half), BF),
            jax.ShapeDtypeStruct((tokens, columns), BF),
            jax.ShapeDtypeStruct((tokens, columns), BF),
            jax.ShapeDtypeStruct((2 * HD, tokens), BF),
        ]
        if not last:
            shapes.append(jax.ShapeDtypeStruct((1, half), F32))
        extra = [gain_before] if last else []
        return pl.pallas_call(
            functools.partial(attend_body, {**plan, "outs": len(shapes)}, len(pieces)),
            out_shape=shapes[:2] + [pltpu.HBM(shape.shape, shape.dtype) for shape in shapes[2:]],
            in_specs=[SMEM] + [VMEM] * (5 + len(pieces) + len(extra)),
            out_specs=[VMEM] * 2 + [HBM] * (len(shapes) - 2),
            scratch_shapes=[pltpu.VMEM(shape.shape, shape.dtype) for shape in shapes[2:]]
            + [pltpu.SemaphoreType.DMA((len(shapes) - 2,))],
            compiler_params=PARAMS,
        )(core, *pieces, stash, norm_gain, query_mat, kv_mat, output_mat, *extra)

    core = (me % 2).astype(jnp.int32).reshape(1)

    def reduce_blocks(mine, other, beside=None):
        got = lax.ppermute(other, "tp", swap_cores)
        chip = (mine.astype(F32) + got.astype(F32)).astype(BF)
        if beside is not None:
            chip, beside = lax.optimization_barrier((chip, beside))
            beside = exchange(beside)
        received = lax.all_to_all(
            chip, "tp", split_axis=0, concat_axis=0, axis_index_groups=same_core, tiled=True
        )
        return jnp.sum(received.astype(F32), axis=0), beside

    def reduce_kv(blocks):
        parts = blocks.reshape(2, 2, HD // 2, -1)
        low, high = parts[:, 0], parts[:, 1]
        got = lax.ppermute(jnp.where(even, high, low), "tp", swap_cores)
        chip = (jnp.where(even, low, high).astype(F32) + got.astype(F32)).astype(BF)
        sends = (
            jnp.where(second_chip, chip[1], chip[0]),
            jnp.where(second_chip, chip[0], chip[1]),
        )
        arrived = [
            lax.ppermute(send, "tp", [(b, a) for a, b in route])
            for send, route in zip(sends, kv_routes)
        ]
        return (arrived[0].astype(F32) + arrived[1].astype(F32)).astype(BF)

    last = sections // 2 - 1
    ahead = [(i, i + 1) for i in range(last)] + [
        (sections - 1 - i, sections - 2 - i) for i in range(last)
    ]
    behind = [(b, a) for a, b in ahead]
    first_layer = (section == 0) | (section == sections - 1)
    last_layer = (section == last) | (section == last + 1)

    gathered = gather(held)
    kept_arrays = tuple(range(1, 2 + ticks))
    groups = [((0, 2), 1)] + [((2 + k,), None) for k in range(1, ticks)]
    projected, (cots, *stash) = project(gathered, groups, kept_arrays, near=(2,))
    (message, own_x), later = projected[0], projected[1:]
    got_x = exchange(message)
    all_cots = [cots]
    act_rows, cot_rows = held[0], held[1]
    gain_total = None
    out_rows, back_rows = [], []
    all_normed, all_query_back, all_kv_back, all_mixed = [], [], [], []
    for k in range(ticks):
        first = k == 0
        plan = {
            "last": k + 1 == ticks,
            "rows": rows,
            "count_x": 2 if first else 1,
            "place_s": 1 if first else 0,
            "count_s": 2 if first else 1,
            "cot_s": first,
        }
        mine, other, normed, query_back, mixed, kv_back, *rest = attend(
            plan,
            (own_x, got_x) if first else (own_x, got_x, own_s, got_s),
            stash[k],
            gain_total,
        )
        if k + 1 < ticks:
            gain_total = rest[0] if gain_total is None else gain_total + rest[0]
        message_s = None if k + 1 == ticks else later[k][0]
        total, arrived_s = reduce_blocks(mine, other, message_s)
        layer_out = (act_rows.astype(F32) + total[:rows, :half]).astype(BF)
        back_input = (cot_rows.astype(F32) + total[rows:, :half]).astype(BF)
        out_rows.append(layer_out)
        back_rows.append(back_input)
        all_kv_back.append(kv_back)
        all_normed.append(normed)
        all_query_back.append(query_back)
        all_mixed.append(mixed)
        if k + 1 < ticks:
            f = layer_out.reshape(2, 2, row_count, half)
            b = back_input.reshape(2, 2, row_count, half)
            going_up = jnp.stack([f[0, 0], f[1, 1], b[1, 0], b[0, 1]])
            going_down = jnp.stack([f[1, 0], f[0, 1], b[0, 0], b[1, 1]])
            going_up, going_down = lax.optimization_barrier((going_up, going_down))
            from_below = lax.ppermute(going_up, "section", ahead)
            from_above = lax.ppermute(going_down, "section", behind)
            from_below, from_above, arrived_s = lax.optimization_barrier(
                (from_below, from_above, arrived_s)
            )
            fresh = jnp.stack(
                [fresh_acts[0, k], fresh_acts[1, k], fresh_grads[0, k], fresh_grads[1, k]]
            )
            fresh = halves(fresh)[0]
            lo = jnp.where(first_layer, fresh, from_below)
            hi = jnp.where(last_layer, going_up, from_above)
            act_rows = jnp.concatenate([lo[0], hi[1], hi[0], lo[1]], axis=0)
            cot_rows = jnp.concatenate([hi[2], lo[3], lo[2], hi[3]], axis=0)
            entering = jnp.stack([act_rows, cot_rows])
            own_s, got_s = later[k][1], arrived_s
            act_rows, cot_rows = entering[0], entering[1]
            moved = gather(entering)
            ((message, own_x),), (cots,) = project(moved, [((0,), 1)], (1,))
            all_cots.append(cots)
            got_x = exchange(message)

    normed = jnp.concatenate(all_normed, axis=0)
    total, *late = lax.optimization_barrier((total, *all_query_back, *all_mixed))
    all_query_back, all_mixed = late[:ticks], late[ticks:]
    grad_query = t_mm(normed, jnp.concatenate(all_query_back, axis=0)).astype(BF)
    grad_keyval = mm(reduce_kv(jnp.concatenate(all_kv_back, axis=1)), normed).astype(BF).T
    grad_output = t_mm(
        jnp.concatenate(all_cots, axis=0), jnp.concatenate(all_mixed, axis=0)
    ).astype(BF)
    gain_lanes = total[:, half:]
    grad_gain = (gain_lanes[:rows] + gain_lanes[rows:]).astype(BF).reshape(half)

    leaving = jnp.stack(out_rows + back_rows).reshape(2 * ticks, 2, 2 * row_count, half)
    lo_rows, hi_rows = leaving[:, 0], leaving[:, 1]
    mine, theirs = jnp.where(lower, lo_rows, hi_rows), jnp.where(lower, hi_rows, lo_rows)
    returned = lax.ppermute(theirs, "section", mirror)
    whole = jnp.concatenate(
        [jnp.where(lower, mine, returned), jnp.where(lower, returned, mine)], axis=2
    ).reshape(2, ticks, 2, row_count, width)
    whole = whole.transpose(0, 2, 1, 3, 4)
    return (
        whole[0][None],
        whole[1][None],
        grad_query[None],
        grad_keyval[None],
        grad_output[None],
        grad_gain[None],
    )


def solution(mesh):
    in_specs = (
        P("section", None, "tp", None),
        P(None, None, "tp", None),
        P("section", None, None, "tp", None),
        P("section", None, "tp", None),
        P(None, None, "tp", None),
        P("section", None),
        P("section", None, "tp"),
        P("section", None, "tp"),
        P("section", "tp", None),
    )
    out_specs = (
        P("section", None, None, "tp", None),
        P("section", None, None, "tp", None),
        P("section", None, "tp"),
        P("section", None, "tp"),
        P("section", None, "tp"),
        P("section", None),
    )
    return jax.shard_map(
        on_device, mesh=mesh, in_specs=in_specs, out_specs=out_specs, check_vma=False
    )
```

```python
import functools
import math

import jax
import jax.numpy as jnp
from jax import lax
from jax.experimental import pallas as pl
from jax.experimental.pallas import tpu as pltpu
from jax.sharding import PartitionSpec as P

HD = 128
KVH = 4
EPSILON = 1e-05
BF = jnp.bfloat16
F32 = jnp.float32


def mm(left, right, dims=((1,), (0,))):
    return lax.dot_general(left, right, (dims, ((), ())), preferred_element_type=F32)


def mm_t(left, right):
    return mm(left, right, ((1,), (1,)))


def t_mm(left, right):
    return mm(left, right, ((0,), (0,)))


def pair_mask(tokens, row_count):
    def parts(axis):
        i = lax.broadcasted_iota(jnp.int32, (tokens, tokens), axis)
        group = (i // row_count) % 4
        return group, (i // (4 * row_count)) * row_count + i % row_count

    (query_group, query_time), (key_group, key_time) = parts(0), parts(1)
    return (query_group == key_group) & (key_time <= query_time)


def array_of(gathered_ref, index, rows):
    part = gathered_ref[...].astype(F32)[:, index * rows : (index + 1) * rows]
    return part.reshape(part.shape[0] * rows, part.shape[2])


def lane_sum(block, lanes):
    lane = lax.broadcasted_iota(jnp.int32, block.shape, 1)
    chosen = functools.reduce(jnp.logical_or, [lane == i for i in lanes])
    return jnp.sum(jnp.where(chosen, block, 0.0), axis=1, keepdims=True)


def project_body(groups, kept_arrays, far, rows, gathered, gain, query_mat, kv_mat, output_mat, *rest):
    results, buffers, sems = rest[: len(far)], rest[len(far) : -1], rest[-1]
    places = [i for i, is_far in enumerate(far) if is_far]
    outs = [buffers[places.index(i)] if is_far else results[i] for i, is_far in enumerate(far)]
    copies = []

    def send(index):
        if far[index]:
            place = places.index(index)
            copies.append(pltpu.make_async_copy(buffers[place], results[index], sems.at[place]))
            copies[-1].start()

    for i, kept_array in enumerate(kept_arrays):
        index = 2 * len(groups) + i
        outs[index][...] = array_of(gathered, kept_array, rows).astype(BF)
        send(index)
    gain_row = gain[...].astype(F32)
    for index, (acts, cot) in enumerate(groups):
        message, own = outs[2 * index], outs[2 * index + 1]
        tokens = own.shape[0]
        at = 0
        squares = []
        for act in acts:
            wide = array_of(gathered, act, rows)
            scaled = (wide * gain_row).astype(BF)
            squares.append(jnp.sum(wide * wide, axis=1, keepdims=True))
            for part in (mm(scaled, query_mat[...]), mm_t(scaled, kv_mat[...])):
                own[:, at : at + part.shape[1]] = part
                message[:, at : at + part.shape[1]] = part.astype(BF)
                at += part.shape[1]
        if cot is not None:
            part = mm_t(array_of(gathered, cot, rows).astype(BF), output_mat[...])
            own[:, at : at + part.shape[1]] = part
            message[:, at : at + part.shape[1]] = part.astype(BF)
            at += part.shape[1]
        lane = lax.broadcasted_iota(jnp.int32, (tokens, HD), 1)
        kept = jnp.zeros((tokens, HD), F32)
        sent = jnp.zeros((tokens, HD), F32)
        for i, square in enumerate(squares):
            high = square.astype(BF).astype(F32)
            kept = jnp.where(lane == i, square, kept)
            sent = jnp.where(lane == i, high, sent)
            sent = jnp.where(lane == len(squares) + i, square - high, sent)
        own[:, at : at + HD] = kept
        message[:, at : at + HD] = sent.astype(BF)
        send(2 * index)
        send(2 * index + 1)
    for copy in copies:
        copy.wait()


def stack_heads(columns):
    return jnp.concatenate([columns[:, i : i + HD] for i in range(0, columns.shape[1], HD)], axis=0)


def unstack_heads(stacked, tokens):
    return jnp.concatenate(
        [stacked[i : i + tokens] for i in range(0, stacked.shape[0], tokens)], axis=1
    )


def softmax_of(stacked, keys, mask):
    scores = mm_t(stacked, keys) / math.sqrt(HD)
    scores = jnp.where(mask, scores, -jnp.inf)
    weights = jnp.exp(scores - jnp.max(scores, axis=1, keepdims=True))
    return weights / jnp.sum(weights, axis=1, keepdims=True)


def attend_body(
    plan, pieces, core, own_x, got_x, *rest
):
    last = plan["last"]
    own_s, got_s = (own_x, got_x) if pieces == 2 else rest[: pieces - 2]
    stash, gain, query_mat, kv_mat, output_mat, *rest = rest[pieces - 2 :]
    if last:
        gain_before, rest = rest[0], rest[1:]
    outs, sems = rest[: plan["outs"]], rest[-1]
    block, other_block = outs[:2]
    leaving = []

    def leave(index, value):
        buffer = rest[plan["outs"] + index - 2]
        buffer[...] = value
        copy = pltpu.make_async_copy(buffer, outs[index], sems.at[index - 2])
        copy.start()
        leaving.append(copy)
    rows, columns = plan["rows"], query_mat.shape[1]
    shards = 2 * block.shape[0]
    tokens, half = shards * rows, query_mat.shape[0]
    eval_columns = columns + 2 * HD
    heads = columns // HD

    def total(own, got, at, size):
        return own[:, at : at + size] + got[:, at : at + size].astype(F32)

    def projected(own, got, place, count, has_cot):
        at = count * eval_columns + (columns if has_cot else 0)
        square = lane_sum(total(own, got, at, HD), (place, count + place))
        inverse = lax.rsqrt(square / (2 * half) + EPSILON)
        start = place * eval_columns
        queries = total(own, got, start, columns) * inverse
        keyvals = total(own, got, start + columns, 2 * HD) * inverse
        return queries, keyvals, inverse

    mask = pair_mask(tokens, rows // 4)
    mask = jnp.concatenate([mask.astype(jnp.int32)] * heads, axis=0) == 1

    queries, keyvals, _ = projected(own_x, got_x, 0, plan["count_x"], True)
    keys, values = keyvals[:, :HD].astype(BF), keyvals[:, HD:].astype(BF)
    probs = softmax_of(stack_heads(queries).astype(BF), keys, mask)
    mixed = unstack_heads(mm(probs.astype(BF), values), tokens).astype(BF)
    out_part = mm(mixed, output_mat[...])

    back_mixed = total(own_x, got_x, plan["count_x"] * eval_columns, columns)
    queries, keyvals, inverse = projected(
        own_s, got_s, plan["place_s"], plan["count_s"], plan["cot_s"]
    )
    keys, values = keyvals[:, :HD].astype(BF), keyvals[:, HD:].astype(BF)
    stacked = stack_heads(queries).astype(BF)
    probs = softmax_of(stacked, keys, mask)
    leave(4, unstack_heads(mm(probs.astype(BF), values), tokens).astype(BF))
    back = stack_heads(back_mixed).astype(BF)
    back_probs = mm_t(back, values)
    inner = jnp.sum(probs * back_probs, axis=1, keepdims=True)
    back_scores = probs * (back_probs - inner) / math.sqrt(HD)
    query_back = unstack_heads(mm(back_scores.astype(BF), keys), tokens).astype(BF)
    leave(3, query_back)
    key_back = mm(back_scores.T.astype(BF), stacked)
    value_back = mm(probs.T.astype(BF), back)
    keyval_back = jnp.concatenate([key_back, value_back], axis=1).astype(BF)
    leave(5, jnp.concatenate([key_back.T, value_back.T], axis=0).astype(BF))

    back_normed = mm_t(query_back, query_mat[...]) + mm(keyval_back, kv_mat[...])
    along = jnp.sum(query_back.astype(F32) * queries, axis=1, keepdims=True) + jnp.sum(
        keyval_back.astype(F32) * keyvals, axis=1, keepdims=True
    )
    gain_row = gain[...].astype(F32)
    unit = stash[...].astype(F32) * inverse
    leave(2, (unit * gain_row).astype(BF))
    back_part = inverse * (back_normed * gain_row - unit * (along / (2 * half)))
    gain_part = jnp.sum(back_normed * unit, axis=0, keepdims=True)

    both = jnp.concatenate(
        [out_part.reshape(shards, rows, half), back_part.reshape(shards, rows, half)], axis=1
    )
    both = both.reshape(shards // 2, 2, 2 * rows, half)
    for target, parity in ((block, 0), (other_block, 1)):
        part = jnp.where(core[0] == parity, both[:, 0], both[:, 1])
        target[:, :, :half] = part.astype(BF)

    if last:
        gain_part = gain_part + gain_before[...]
        high = gain_part.astype(BF).astype(F32)
        width = half // rows
        spread = jnp.concatenate(
            [part[:, i * width : (i + 1) * width] for part in (high, gain_part - high) for i in range(rows)],
            axis=0,
        ).astype(BF)
        for d in range(shards // 2):
            block[d, :, half:] = spread
            other_block[d, :, half:] = spread
    else:
        leave(6, gain_part)
    for copy in leaving:
        copy.wait()


VMEM = pl.BlockSpec(memory_space=pltpu.VMEM)
SMEM = pl.BlockSpec(memory_space=pltpu.SMEM)
HBM = pl.BlockSpec(memory_space=pltpu.HBM)
PARAMS = pltpu.CompilerParams(vmem_limit_bytes=24 * 2**20)


def on_device(
    carried_acts,
    fresh_acts,
    stashed_acts,
    carried_grads,
    fresh_grads,
    norm_gain,
    query_weight,
    keyval_weight,
    output_weight,
):
    sections = lax.axis_size("section")
    shards = lax.axis_size("tp")
    section = lax.axis_index("section")
    me = lax.axis_index("tp")
    lower = section < sections // 2
    ticks = stashed_acts.shape[2]
    width = carried_acts.shape[3]
    half = width // 2
    row_count = carried_acts.shape[2]
    rows = 4 * row_count
    tokens = rows * shards
    query_mat, output_mat = query_weight[0], output_weight[0]
    columns = query_mat.shape[1]
    mirror = [(i, sections - 1 - i) for i in range(sections)]
    kv_group = shards // KVH

    def halves(whole):
        first, second = whole[..., :half], whole[..., half:]
        return jnp.where(lower, first, second), jnp.where(lower, second, first)

    entering = jnp.stack(
        [carried_acts[0], carried_grads[0]] + [stashed_acts[0, :, k] for k in range(ticks)]
    ).reshape(ticks + 2, 2 * row_count, width)
    own, other = halves(entering)
    arrived = lax.ppermute(other, "section", mirror)
    held = jnp.concatenate(
        [jnp.where(lower, own, arrived), jnp.where(lower, arrived, own)], axis=1
    )

    kv_own = keyval_weight[0].T
    sources = [[2 * j, 2 * j + 1, shards // 2 + 2 * j, shards // 2 + 2 * j + 1] for j in range(KVH)]
    kv_routes = [
        [
            (sources[j][(i + 2 * k) % kv_group], kv_group * j + i)
            for j in range(KVH)
            for i in range(kv_group)
        ]
        for k in range(2)
    ]
    swap_cores = [(i, i ^ 1) for i in range(shards)]
    fetched = [lax.ppermute(kv_own, "tp", route) for route in kv_routes]
    second_chip = (me // 2) % 2 == 1
    mine = jnp.stack(
        [
            jnp.where(second_chip, fetched[1], fetched[0]),
            jnp.where(second_chip, fetched[0], fetched[1]),
        ]
    )
    swapped = lax.ppermute(mine, "tp", swap_cores)
    even = me % 2 == 0
    kv_mat = jnp.stack(
        [jnp.where(even, mine, swapped), jnp.where(even, swapped, mine)], axis=1
    ).reshape(2 * HD, half)

    same_core = [[2 * chip + core for chip in range(shards // 2)] for core in range(2)]

    def gather(local):
        count, chips = local.shape[0], shards // 2
        spread = jnp.broadcast_to(local.reshape(1, count * rows, half), (chips, count * rows, half))
        mine = lax.all_to_all(
            spread, "tp", split_axis=0, concat_axis=0, axis_index_groups=same_core, tiled=True
        )
        other = lax.ppermute(mine, "tp", swap_cores)
        both = jnp.stack(
            [jnp.where(even, mine, other), jnp.where(even, other, mine)], axis=1
        )
        return both.reshape(shards, count * rows, half)

    eval_columns = columns + 2 * HD

    def project(gathered, groups, kept_arrays, near=()):
        shapes, far = [], []
        for i, (acts, cot) in enumerate(groups):
            size = len(acts) * eval_columns + (0 if cot is None else columns) + HD
            shapes += [((tokens, size), BF), ((tokens, size), F32)]
            far += [i > 0] * 2
        shapes += [((tokens, half), BF)] * len(kept_arrays)
        far += [kept_array not in near for kept_array in kept_arrays]
        outs = pl.pallas_call(
            functools.partial(project_body, groups, kept_arrays, far, rows),
            out_shape=[
                pltpu.HBM(*shape) if is_far else jax.ShapeDtypeStruct(*shape)
                for shape, is_far in zip(shapes, far)
            ],
            in_specs=[VMEM] * 5,
            out_specs=[HBM if is_far else VMEM for is_far in far],
            scratch_shapes=[pltpu.VMEM(*shape) for shape, is_far in zip(shapes, far) if is_far]
            + [pltpu.SemaphoreType.DMA((sum(far),))],
            compiler_params=PARAMS,
        )(gathered, norm_gain, query_mat, kv_mat, output_mat)
        pairs = [(outs[2 * i], outs[2 * i + 1]) for i in range(len(groups))]
        return pairs, outs[2 * len(groups) :]

    def exchange(message):
        return lax.ppermute(message, "section", mirror)

    def attend(plan, pieces, stash, gain_before):
        last = plan["last"]
        lanes = half + (half // rows if last else 0)
        shapes = [
            jax.ShapeDtypeStruct((shards // 2, 2 * rows, lanes), BF),
            jax.ShapeDtypeStruct((shards // 2, 2 * rows, lanes), BF),
            jax.ShapeDtypeStruct((tokens, half), BF),
            jax.ShapeDtypeStruct((tokens, columns), BF),
            jax.ShapeDtypeStruct((tokens, columns), BF),
            jax.ShapeDtypeStruct((2 * HD, tokens), BF),
        ]
        if not last:
            shapes.append(jax.ShapeDtypeStruct((1, half), F32))
        extra = [gain_before] if last else []
        return pl.pallas_call(
            functools.partial(attend_body, {**plan, "outs": len(shapes)}, len(pieces)),
            out_shape=shapes[:2] + [pltpu.HBM(shape.shape, shape.dtype) for shape in shapes[2:]],
            in_specs=[SMEM] + [VMEM] * (5 + len(pieces) + len(extra)),
            out_specs=[VMEM] * 2 + [HBM] * (len(shapes) - 2),
            scratch_shapes=[pltpu.VMEM(shape.shape, shape.dtype) for shape in shapes[2:]]
            + [pltpu.SemaphoreType.DMA((len(shapes) - 2,))],
            compiler_params=PARAMS,
        )(core, *pieces, stash, norm_gain, query_mat, kv_mat, output_mat, *extra)

    core = (me % 2).astype(jnp.int32).reshape(1)

    def reduce_blocks(mine, other, beside=None):
        got = lax.ppermute(other, "tp", swap_cores)
        chip = (mine.astype(F32) + got.astype(F32)).astype(BF)
        if beside is not None:
            chip, beside = lax.optimization_barrier((chip, beside))
            beside = exchange(beside)
        received = lax.all_to_all(
            chip, "tp", split_axis=0, concat_axis=0, axis_index_groups=same_core, tiled=True
        )
        return jnp.sum(received.astype(F32), axis=0), beside

    def reduce_kv(blocks):
        parts = blocks.reshape(2, 2, HD // 2, -1)
        low, high = parts[:, 0], parts[:, 1]
        got = lax.ppermute(jnp.where(even, high, low), "tp", swap_cores)
        chip = (jnp.where(even, low, high).astype(F32) + got.astype(F32)).astype(BF)
        sends = (
            jnp.where(second_chip, chip[1], chip[0]),
            jnp.where(second_chip, chip[0], chip[1]),
        )
        arrived = [
            lax.ppermute(send, "tp", [(b, a) for a, b in route])
            for send, route in zip(sends, kv_routes)
        ]
        return (arrived[0].astype(F32) + arrived[1].astype(F32)).astype(BF)

    last = sections // 2 - 1
    ahead = [(i, i + 1) for i in range(last)] + [
        (sections - 1 - i, sections - 2 - i) for i in range(last)
    ]
    behind = [(b, a) for a, b in ahead]
    first_layer = (section == 0) | (section == sections - 1)
    last_layer = (section == last) | (section == last + 1)

    gathered = gather(held)
    kept_arrays = tuple(range(1, 2 + ticks))
    groups = [((0, 2), 1)] + [((2 + k,), None) for k in range(1, ticks)]
    projected, (cots, *stash) = project(gathered, groups, kept_arrays, near=(2,))
    (message, own_x), later = projected[0], projected[1:]
    got_x = exchange(message)
    all_cots = [cots]
    act_rows, cot_rows = held[0], held[1]
    gain_total = None
    out_rows, back_rows = [], []
    all_normed, all_query_back, all_kv_back, all_mixed = [], [], [], []
    for k in range(ticks):
        first = k == 0
        plan = {
            "last": k + 1 == ticks,
            "rows": rows,
            "count_x": 2 if first else 1,
            "place_s": 1 if first else 0,
            "count_s": 2 if first else 1,
            "cot_s": first,
        }
        mine, other, normed, query_back, mixed, kv_back, *rest = attend(
            plan,
            (own_x, got_x) if first else (own_x, got_x, own_s, got_s),
            stash[k],
            gain_total,
        )
        if k + 1 < ticks:
            gain_total = rest[0] if gain_total is None else gain_total + rest[0]
        message_s = None if k + 1 == ticks else later[k][0]
        total, arrived_s = reduce_blocks(mine, other, message_s)
        layer_out = (act_rows.astype(F32) + total[:rows, :half]).astype(BF)
        back_input = (cot_rows.astype(F32) + total[rows:, :half]).astype(BF)
        out_rows.append(layer_out)
        back_rows.append(back_input)
        all_kv_back.append(kv_back)
        all_normed.append(normed)
        all_query_back.append(query_back)
        all_mixed.append(mixed)
        if k + 1 < ticks:
            f = layer_out.reshape(2, 2, row_count, half)
            b = back_input.reshape(2, 2, row_count, half)
            going_up = jnp.stack([f[0, 0], f[1, 1], b[1, 0], b[0, 1]])
            going_down = jnp.stack([f[1, 0], f[0, 1], b[0, 0], b[1, 1]])
            going_up, going_down = lax.optimization_barrier((going_up, going_down))
            from_below = lax.ppermute(going_up, "section", ahead)
            from_above = lax.ppermute(going_down, "section", behind)
            from_below, from_above, arrived_s = lax.optimization_barrier(
                (from_below, from_above, arrived_s)
            )
            fresh = jnp.stack(
                [fresh_acts[0, k], fresh_acts[1, k], fresh_grads[0, k], fresh_grads[1, k]]
            )
            fresh = halves(fresh)[0]
            lo = jnp.where(first_layer, fresh, from_below)
            hi = jnp.where(last_layer, going_up, from_above)
            act_rows = jnp.concatenate([lo[0], hi[1], hi[0], lo[1]], axis=0)
            cot_rows = jnp.concatenate([hi[2], lo[3], lo[2], hi[3]], axis=0)
            entering = jnp.stack([act_rows, cot_rows])
            own_s, got_s = later[k][1], arrived_s
            act_rows, cot_rows = entering[0], entering[1]
            moved = gather(entering)
            ((message, own_x),), (cots,) = project(moved, [((0,), 1)], (1,))
            all_cots.append(cots)
            got_x = exchange(message)

    normed = jnp.concatenate(all_normed, axis=0)
    total, *late = lax.optimization_barrier((total, *all_query_back, *all_mixed))
    all_query_back, all_mixed = late[:ticks], late[ticks:]
    grad_query = t_mm(normed, jnp.concatenate(all_query_back, axis=0)).astype(BF)
    grad_keyval = mm(reduce_kv(jnp.concatenate(all_kv_back, axis=1)), normed).astype(BF).T
    grad_output = t_mm(
        jnp.concatenate(all_cots, axis=0), jnp.concatenate(all_mixed, axis=0)
    ).astype(BF)
    gain_lanes = total[:, half:]
    grad_gain = (gain_lanes[:rows] + gain_lanes[rows:]).astype(BF).reshape(half)

    leaving = jnp.stack(out_rows + back_rows).reshape(2 * ticks, 2, 2 * row_count, half)
    lo_rows, hi_rows = leaving[:, 0], leaving[:, 1]
    mine, theirs = jnp.where(lower, lo_rows, hi_rows), jnp.where(lower, hi_rows, lo_rows)
    returned = lax.ppermute(theirs, "section", mirror)
    whole = jnp.concatenate(
        [jnp.where(lower, mine, returned), jnp.where(lower, returned, mine)], axis=2
    ).reshape(2, ticks, 2, row_count, width)
    whole = whole.transpose(0, 2, 1, 3, 4)
    return (
        whole[0][None],
        whole[1][None],
        grad_query[None],
        grad_keyval[None],
        grad_output[None],
        grad_gain[None],
    )


def solution(mesh):
    in_specs = (
        P("section", None, "tp", None),
        P(None, None, "tp", None),
        P("section", None, None, "tp", None),
        P("section", None, "tp", None),
        P(None, None, "tp", None),
        P("section", None),
        P("section", None, "tp"),
        P("section", None, "tp"),
        P("section", "tp", None),
    )
    out_specs = (
        P("section", None, None, "tp", None),
        P("section", None, None, "tp", None),
        P("section", None, "tp"),
        P("section", None, "tp"),
        P("section", None, "tp"),
        P("section", None),
    )
    return jax.shard_map(
        on_device, mesh=mesh, in_specs=in_specs, out_specs=out_specs, check_vma=False
    )
```
